512 devices in a mesh: dom: 128 (over y, z, core), feat: 4 (over x).
Axes of the slice: x: 4, y: 8, z: 8, core: 2. Of those that a mesh axis runs over, the one named last changes fastest.
Arguments:
- x_t: bfloat16 [128, 65536], P('feat', 'dom'), may hold values from -24 to 24
- w_self: bfloat16 [128, 256], P('feat'), may hold values from -0.5 to 0.5
- w_neigh: bfloat16 [128, 256], P('feat'), may hold values from -0.5 to 0.5
- in_adj: bfloat16 [1536, 128, 128], P('dom'), may hold values from 0 to 0.046875
- in_rows: int32 [1536], P('dom'), may hold values from 0 to 3
- in_cols: int32 [1536], P('dom'), may hold values from 0 to 3
- bnd_adj: bfloat16 [1536, 128, 128], P('dom'), may hold values from 0 to 0.046875
- bnd_send: int32 [1536], P('dom'), may hold values from 0 to 3
- bnd_rows: int32 [1536], P('dom'), may hold values from 0 to 3
- grad_out: bfloat16 [256, 65536], P('feat', 'dom'), may hold values from -6 to 6
Outputs:
- y_t: bfloat16 [256, 65536], P('feat', 'dom')
- grad_x: float32 [128, 65536], P('feat', 'dom')
- grad_ws: float32 [128, 256], P('feat')
- grad_wn: float32 [128, 256], P('feat')
The draws below stay inside these ranges and needn't reach their ends.
Inputs may be any that keep to these rules, and one draw needn't show every extreme that they name: `in_rows`: a tile index within one partition. `in_cols`: a tile index within one partition. `bnd_send`: a tile index within the sending partition. `bnd_rows`: a tile index within the receiving partition.
All inputs are finite; a program needn't handle non-finite values.
Results may differ from the reference program's by a relative error of at most 0.0054.
Values may be sent and summed in bfloat16 or wider, within the bound.
No kernel may reach another device: no remote copies, remote signals or barrier semaphores. Data moves between devices by JAX's collectives and lax.ppermute only.
A program may use at most 64 MiB of HBM per device.

```python
import functools
import math
import jax
import jax.numpy as jnp
from jax import lax

F_IN = 128
F_HID = 256
TILE = 128
TILES_DEV = 4
ROUNDS = 3
BT = 4
KIN = 12
NODES = 65536
IN_TOTAL = 1536
BND_TOTAL = 1536
N_DOM = 128


def draw_x_t(key, part):
    subkeys = jax.random.split(key, 3)
    feature_scale = jnp.exp(jax.random.uniform(subkeys[1], (F_IN, 1), jnp.float32, -0.8, 0.8))
    node_scale = jnp.exp(jax.random.uniform(subkeys[2], (1, NODES), jnp.float32, -0.8, 0.8))
    raw_values = jax.random.normal(subkeys[0], (F_IN, NODES), jnp.float32)
    return jnp.clip(raw_values * feature_scale * node_scale, -24.0, 24.0).astype(jnp.bfloat16)


def plant(array, own_key, low, top_value):
    shape = array.shape
    spot = [jax.random.randint(jax.random.fold_in(own_key, axis), (), 0, shape[axis]) for axis in range(len(shape))]
    array = array.at[tuple(spot)].set(low)
    longest = shape.index(max(shape))
    spot[longest] = (spot[longest] + 1) % shape[longest]
    return array.at[tuple(spot)].set(top_value)


def block_scale(rng, dims, cuts, smallest, largest):
    factor_of = 1.0
    for position, parts in cuts:
        steps = jax.random.uniform(jax.random.fold_in(jax.random.fold_in(rng, 6), position), (parts,), jnp.float32, smallest / len(cuts), largest / len(cuts))
        factor_of = factor_of * jnp.repeat(jnp.exp(steps), dims[position] // parts).reshape((-1,) + (1,) * (len(dims) - 1 - position))
    return factor_of


def noise(key, dims, scale, limit, cuts=(), kind=jnp.bfloat16):
    gain = block_scale(key, dims, cuts, -0.22, 0.18) if cuts else 1.0
    result = jax.random.normal(key, dims, jnp.float32) * scale * gain
    return jnp.minimum(jnp.maximum(result, -limit), limit).astype(kind)


def setup_inputs(seed: int = 0) -> dict:
    arg_keys = jax.random.split(jax.random.key(seed), 11)
    return {
        "x_t": draw_x_t(jax.random.fold_in(arg_keys[10], 71), 0),
        "w_self": noise(arg_keys[1], (F_IN, F_HID), F_IN ** -0.5, 0.5, ((0, 4),)),
        "w_neigh": noise(arg_keys[2], (F_IN, F_HID), F_IN ** -0.5, 0.5, ((0, 4),)),
        "in_adj": jnp.clip(0.046875 * jax.random.uniform(arg_keys[3], (IN_TOTAL, TILE, TILE), jnp.float32) ** block_scale(arg_keys[3], (IN_TOTAL, TILE, TILE), ((0, 128),), -0.2, 0.2), 0.0, 0.046875).astype(jnp.bfloat16),
        "in_rows": plant(jax.random.randint(arg_keys[4], (IN_TOTAL,), 0, TILES_DEV), jax.random.fold_in(arg_keys[4], 1), 0, TILES_DEV - 1).astype(jnp.int32),
        "in_cols": plant(jax.random.randint(arg_keys[5], (IN_TOTAL,), 0, TILES_DEV), jax.random.fold_in(arg_keys[5], 1), 0, TILES_DEV - 1).astype(jnp.int32),
        "bnd_adj": jnp.clip(0.046875 * jax.random.uniform(arg_keys[6], (BND_TOTAL, TILE, TILE), jnp.float32) ** block_scale(arg_keys[6], (BND_TOTAL, TILE, TILE), ((0, 128),), -0.2, 0.2), 0.0, 0.046875).astype(jnp.bfloat16),
        "bnd_send": plant(jax.random.randint(arg_keys[7], (BND_TOTAL,), 0, TILES_DEV), jax.random.fold_in(arg_keys[7], 1), 0, TILES_DEV - 1).astype(jnp.int32),
        "bnd_rows": plant(jax.random.randint(arg_keys[8], (BND_TOTAL,), 0, TILES_DEV), jax.random.fold_in(arg_keys[8], 1), 0, TILES_DEV - 1).astype(jnp.int32),
        "grad_out": noise(arg_keys[9], (F_HID, NODES), 1.0, 6.0, ((0, 4), (1, 128))),
    }


HIGHEST = lax.Precision.HIGHEST
epsilon = 1e-05

def round_bits(levels):
    return [(number + 1) * levels // ROUNDS - 1 for number in range(ROUNDS)]

def segment_onehot(targets, extent):
    return (targets[None, :] == jnp.arange(extent, dtype=jnp.int32)[:, None]).astype(jnp.float32)

def tile_apply(source, weights, take_from, put_into, flipped):
    picked = source[:, take_from, :]
    if flipped:
        product = jnp.einsum('fki,kij->fkj', picked, weights, precision=HIGHEST)
    else:
        product = jnp.einsum('fkj,kij->fki', picked, weights, precision=HIGHEST)
    return jnp.einsum('fki,tk->fti', product, segment_onehot(put_into, source.shape[1]), precision=HIGHEST)

def normalize(pre_act, active, cotangent, squares, aligned):
    rscale = lax.rsqrt(squares / F_HID + epsilon)
    output = (active * rscale).astype(jnp.bfloat16)
    grad_act = rscale * cotangent - active * rscale ** 3 * (aligned / F_HID)
    gate_value = jax.nn.sigmoid(pre_act)
    grad_pre = (grad_act * gate_value * (1.0 + pre_act * (1.0 - gate_value))).astype(jnp.bfloat16)
    return (output, grad_pre)

def reference(x_t, w_self, w_neigh, in_adj, in_rows, in_cols, bnd_adj, bnd_send, bnd_rows, grad_out):
    feature_rows = x_t.shape[0]
    blocks = x_t.astype(jnp.float32).reshape(feature_rows, N_DOM, TILES_DEV, TILE)
    inner_adj = in_adj.astype(jnp.float32).reshape(N_DOM, KIN, TILE, TILE)
    inner_rows = in_rows.reshape(N_DOM, KIN)
    inner_cols = in_cols.reshape(N_DOM, KIN)
    outer_adj = bnd_adj.astype(jnp.float32).reshape(N_DOM, ROUNDS, BT, TILE, TILE)
    outer_send = bnd_send.reshape(N_DOM, ROUNDS, BT)
    outer_rows = bnd_rows.reshape(N_DOM, ROUNDS, BT)
    owners = jnp.arange(N_DOM, dtype=jnp.int32)
    tile_ids = jnp.arange(TILES_DEV, dtype=jnp.int32)
    swap_bits = round_bits(N_DOM.bit_length() - 1)
    forward_tiles = jax.vmap(functools.partial(tile_apply, flipped=False), in_axes=(1, 0, 0, 0), out_axes=1)
    inner_sum = forward_tiles(blocks, inner_adj, inner_cols, inner_rows)
    outer_sum = jnp.zeros_like(inner_sum)
    for number, bit_index in enumerate(swap_bits):
        partner = jnp.bitwise_xor(owners, 1 << bit_index)
        source_tiles = outer_send[:, number, :][partner]
        received = blocks[:, partner[:, None], source_tiles, :]
        product = jnp.einsum('fpbj,pbij->fpbi', received, outer_adj[:, number], precision=HIGHEST)
        placing = (outer_rows[:, number, :][:, None, :] == tile_ids[None, :, None]).astype(jnp.float32)
        outer_sum = outer_sum + jnp.einsum('fpbi,ptb->fpti', product, placing, precision=HIGHEST)
    aggregate = (inner_sum + outer_sum).reshape(feature_rows, NODES).astype(jnp.bfloat16)
    pre_act = jnp.dot(w_self.T, x_t, preferred_element_type=jnp.float32)
    pre_act = pre_act + jnp.dot(w_neigh.T, aggregate, preferred_element_type=jnp.float32)
    active = jax.nn.silu(pre_act)
    cotangent = grad_out.astype(jnp.float32)
    squares = lax.optimization_barrier(jnp.sum(active * active, axis=0))
    aligned = lax.optimization_barrier(jnp.sum(cotangent * active, axis=0))
    y_t, grad_pre = normalize(pre_act, active, cotangent, squares, aligned)
    norm_scale = 1.0 / math.sqrt(NODES)
    grad_ws = jnp.dot(x_t, grad_pre.T, preferred_element_type=jnp.float32) * norm_scale
    grad_wn = jnp.dot(aggregate, grad_pre.T, preferred_element_type=jnp.float32) * norm_scale
    self_part = jnp.dot(w_self, grad_pre, preferred_element_type=jnp.float32)
    grad_agg = jnp.dot(w_neigh, grad_pre, preferred_element_type=jnp.float32).astype(jnp.bfloat16)
    grad_blocks = grad_agg.astype(jnp.float32).reshape(feature_rows, N_DOM, TILES_DEV, TILE)
    backward_tiles = jax.vmap(functools.partial(tile_apply, flipped=True), in_axes=(1, 0, 0, 0), out_axes=1)
    back_sum = backward_tiles(grad_blocks, inner_adj, inner_rows, inner_cols)
    for number, bit_index in enumerate(swap_bits):
        partner = jnp.bitwise_xor(owners, 1 << bit_index)
        picked = grad_blocks[:, owners[:, None], outer_rows[:, number, :], :]
        product = jnp.einsum('fqbi,qbij->fqbj', picked, outer_adj[:, number], precision=HIGHEST)
        arriving = product[:, partner]
        placing = (outer_send[:, number, :][:, None, :] == tile_ids[None, :, None]).astype(jnp.float32)
        back_sum = back_sum + jnp.einsum('fpbj,ptb->fptj', arriving, placing, precision=HIGHEST)
    grad_x = self_part + back_sum.reshape(feature_rows, NODES)
    return (y_t, grad_x, grad_ws, grad_wn)
```

```python
import math

import jax
import jax.numpy as jnp
from jax import lax
from jax.experimental import pallas as pl
from jax.experimental.pallas import tpu as pltpu
from jax.sharding import Mesh
from jax.sharding import PartitionSpec as P

F_IN = 128
F_HID = 256
TILE = 128
TILES = 4
ROUNDS = 3
BT = 4
KIN = 12
NODES = 65536
NF = 4
FR = F_IN // NF
HR = F_HID // NF
LOCAL = TILES * TILE
EPS = 1e-05

AXES = ("y2", "yl", "z2", "z1", "z0", "c", "f")
SIZES = (2, 4, 2, 2, 2, 2, 4)
DOM = AXES[:6]
Y = ("y2", "yl")
ZC = ("z2", "z1", "z0", "c")
PAIRS = ("z0", "z2", "y2")

R_AGG, R_X, R_G, R_W = 0, FR, 2 * FR, 2 * FR + HR
ROWS = R_W + FR

SMEM = pl.BlockSpec(memory_space=pltpu.SMEM)
VMEM = pl.BlockSpec(memory_space=pltpu.VMEM)
f32, bf16 = jnp.float32, jnp.bfloat16


def lanes(tile):
    return pl.ds(pl.multiple_of(tile * TILE, TILE), TILE)


def pick_kernel(send, x, *outs):
    for r in range(ROUNDS):
        for b in range(BT):
            outs[r][:, b * TILE : (b + 1) * TILE] = x[:, lanes(send[r * BT + b])]


def agg_kernel(rows, cols, brows, x, r0, r1, r2, adj, badj, g, ws, wn, out, acc):
    nt = (((1,), (1,)), ((), ()))
    acc[...] = jnp.zeros_like(acc)
    for k in range(KIN):
        acc[rows[k]] += lax.dot_general(
            x[:, lanes(cols[k])], adj[k], nt, preferred_element_type=f32
        )
    got = (r0, r1, r2)
    for s in range(ROUNDS * BT):
        b = s % BT
        acc[brows[s]] += lax.dot_general(
            got[s // BT][:, b * TILE : (b + 1) * TILE], badj[s], nt, preferred_element_type=f32
        )
    for i in range(NF):
        for t in range(TILES):
            out[i, R_AGG : R_AGG + FR, t * TILE : (t + 1) * TILE] = acc[t].astype(bf16)
        out[i, R_X : R_X + FR, :] = x[...]
        out[i, R_G : R_G + HR, :] = g[...]
        out[i, R_W : R_W + FR, :F_HID] = ws[...]
        out[i, R_W : R_W + FR, F_HID:] = wn[...]


def node_kernel(me, got, y, gp, wg, lhs, rhs, act_all):
    for i in range(NF):
        lhs[i * FR : (i + 1) * FR, :] = got[i, R_W : R_W + FR, :F_HID]
        lhs[F_IN + i * FR : F_IN + (i + 1) * FR, :] = got[i, R_W : R_W + FR, F_HID:]
        rhs[i * FR : (i + 1) * FR, :] = got[i, R_X : R_X + FR, :]
        rhs[F_IN + i * FR : F_IN + (i + 1) * FR, :] = got[i, R_AGG : R_AGG + FR, :]
    tn = (((0,), (0,)), ((), ()))
    pre = lax.dot_general(lhs[...], rhs[...], tn, preferred_element_type=f32)
    gate = 1.0 / (1.0 + jnp.exp(-pre))
    act = pre * gate
    act_all[...] = act
    g = jnp.concatenate([got[i, R_G : R_G + HR, :] for i in range(NF)], axis=0).astype(f32)
    sq = jnp.sum(act * act, axis=0, keepdims=True)
    al = jnp.sum(g * act, axis=0, keepdims=True)
    rs = lax.rsqrt(sq / F_HID + EPS)
    coef = rs * rs * rs * (al / F_HID)
    grad_act = rs * g - act * coef
    grad = (grad_act * gate * (1.0 + pre * (1.0 - gate))).astype(bf16)
    gp[...] = grad
    f = me[0]
    y[...] = (act_all[pl.ds(pl.multiple_of(f * HR, HR), HR), :] * rs).astype(bf16)
    w = lax.dot_general(
        got[f, R_AGG : R_AGG + 2 * FR, :], grad, (((1,), (1,)), ((), ())), preferred_element_type=f32
    ) * (1.0 / math.sqrt(NODES))
    for j in range(8):
        wg[j] = w[j * 8 : (j + 1) * 8, :]


def back_kernel(rows, cols, brows, gp, ws, wn, adj, badj, base, b0, b1, b2, acc, ga):
    own = jnp.dot(ws[...], gp[...], preferred_element_type=f32)
    grad_agg = jnp.dot(wn[...], gp[...], preferred_element_type=f32).astype(bf16)
    for t in range(TILES):
        acc[t] = own[:, t * TILE : (t + 1) * TILE]
        ga[t] = grad_agg[:, t * TILE : (t + 1) * TILE]
    outs = (b0, b1, b2)
    for s in range(ROUNDS * BT):
        b = s % BT
        outs[s // BT][:, b * TILE : (b + 1) * TILE] = jnp.dot(
            ga[brows[s]], badj[s], preferred_element_type=f32
        ).astype(bf16)
    for k in range(KIN):
        acc[cols[k]] += jnp.dot(ga[rows[k]], adj[k], preferred_element_type=f32)
    for t in range(TILES):
        base[:, t * TILE : (t + 1) * TILE] = acc[t]


def join_kernel(send, base, c0, c1, c2, out):
    out[...] = base[...]
    got = (c0, c1, c2)
    for s in range(ROUNDS * BT):
        b = s % BT
        out[:, lanes(send[s])] += got[s // BT][:, b * TILE : (b + 1) * TILE].astype(f32)


def call(kernel, ins, outs, scratch=(), flops=0, nbytes=1 << 20):
    many = isinstance(outs, tuple)
    return pl.pallas_call(
        kernel,
        out_shape=outs,
        in_specs=[SMEM if i else VMEM for i in ins],
        out_specs=tuple(VMEM for _ in outs) if many else VMEM,
        scratch_shapes=list(scratch),
        cost_estimate=pl.CostEstimate(flops=flops, bytes_accessed=nbytes, transcendentals=0),
    )


def swap(x, axis):
    return lax.ppermute(x, axis, [(0, 1), (1, 0)])


def shards(x, ws, wn, in_adj, in_rows, in_cols, bnd_adj, bnd_send, bnd_rows, g):
    S = jax.ShapeDtypeStruct
    part = S((FR, LOCAL), bf16)
    picked = call(pick_kernel, (1, 0), (part,) * 3)(bnd_send, x)
    got = [swap(picked[r], PAIRS[r]) for r in range(ROUNDS)]
    give = call(
        agg_kernel,
        (1, 1, 1) + (0,) * 9,
        S((NF, ROWS, LOCAL), bf16),
        (pltpu.VMEM((TILES, FR, TILE), f32),),
    )(in_rows, in_cols, bnd_rows, x, *got, in_adj, bnd_adj, g, ws, wn)
    block = lax.all_to_all(give, "f", 0, 0, tiled=True)
    me = lax.axis_index("f").astype(jnp.int32).reshape(1)
    y, gp, wg = call(
        node_kernel,
        (1, 0),
        (S((HR, LOCAL), bf16), S((F_HID, LOCAL), bf16), S((8, 8, F_HID), f32)),
        (
            pltpu.VMEM((2 * F_IN, F_HID), bf16),
            pltpu.VMEM((2 * F_IN, LOCAL), bf16),
            pltpu.VMEM((F_HID, LOCAL), f32),
        ),
    )(me, block)
    wg = lax.all_to_all(wg, Y, 0, 0, tiled=True)
    base, *back = call(
        back_kernel,
        (1, 1, 1) + (0,) * 5,
        (S((FR, LOCAL), f32),) + (part,) * 3,
        (pltpu.VMEM((TILES, FR, TILE), f32), pltpu.VMEM((TILES, FR, TILE), bf16)),
    )(in_rows, in_cols, bnd_rows, gp, ws, wn, in_adj, bnd_adj)
    wg = jnp.broadcast_to(jnp.sum(wg, axis=0), (16, 8, F_HID))
    wg = lax.all_to_all(wg, ZC, 0, 0, tiled=True)
    home = [swap(back[r], PAIRS[r]) for r in range(ROUNDS)]
    wg = jnp.broadcast_to(jnp.sum(wg, axis=0), (8, 8, F_HID))
    wg = lax.all_to_all(wg, Y, 0, 0, tiled=True).reshape(2 * FR, F_HID)
    grad_x = call(join_kernel, (1,) + (0,) * 4, S((FR, LOCAL), f32))(bnd_send, base, *home)
    return y, grad_x, wg[FR:], wg[:FR]


def solution(mesh):
    fine = Mesh(mesh.devices.reshape(SIZES), AXES)
    in_specs = (
        P("f", DOM),
        P("f", None),
        P("f", None),
        P(DOM, None, None),
        P(DOM),
        P(DOM),
        P(DOM, None, None),
        P(DOM),
        P(DOM),
        P("f", DOM),
    )
    out_specs = (P("f", DOM), P("f", DOM), P("f", None), P("f", None))
    return jax.shard_map(shards, mesh=fine, in_specs=in_specs, out_specs=out_specs, check_vma=False)
```

```python
import math

import jax
import jax.numpy as jnp
from jax import lax
from jax.experimental import pallas as pl
from jax.experimental.pallas import tpu as pltpu
from jax.sharding import Mesh
from jax.sharding import PartitionSpec as P

F_IN = 128
F_HID = 256
TILE = 128
TILES = 4
ROUNDS = 3
BT = 4
KIN = 12
NODES = 65536
NF = 4
FR = F_IN // NF
HR = F_HID // NF
LOCAL = TILES * TILE
EPS = 1e-05

AXES = ("y2", "yl", "z2", "z1", "z0", "c", "f")
SIZES = (2, 4, 2, 2, 2, 2, 4)
DOM = AXES[:6]
Y = ("y2", "yl")
ZC = ("z2", "z1", "z0", "c")
PAIRS = ("z0", "z2", "y2")

R_AGG, R_X, R_G, R_W = 0, FR, 2 * FR, 2 * FR + HR
ROWS = R_W + FR

SMEM = pl.BlockSpec(memory_space=pltpu.SMEM)
VMEM = pl.BlockSpec(memory_space=pltpu.VMEM)
f32, bf16 = jnp.float32, jnp.bfloat16


def lanes(tile):
    return pl.ds(pl.multiple_of(tile * TILE, TILE), TILE)


def pick_kernel(send, x, *outs):
    for r in range(ROUNDS):
        for b in range(BT):
            outs[r][:, b * TILE : (b + 1) * TILE] = x[:, lanes(send[r * BT + b])]


def agg_kernel(rows, cols, brows, x, r0, r1, r2, adj, badj, g, ws, wn, out, acc):
    nt = (((1,), (1,)), ((), ()))
    acc[...] = jnp.zeros_like(acc)
    for k in range(KIN):
        acc[rows[k]] += lax.dot_general(
            x[:, lanes(cols[k])], adj[k], nt, preferred_element_type=f32
        )
    got = (r0, r1, r2)
    for s in range(ROUNDS * BT):
        b = s % BT
        acc[brows[s]] += lax.dot_general(
            got[s // BT][:, b * TILE : (b + 1) * TILE], badj[s], nt, preferred_element_type=f32
        )
    for i in range(NF):
        for t in range(TILES):
            out[i, R_AGG : R_AGG + FR, t * TILE : (t + 1) * TILE] = acc[t].astype(bf16)
        out[i, R_X : R_X + FR, :] = x[...]
        out[i, R_G : R_G + HR, :] = g[...]
        out[i, R_W : R_W + FR, :F_HID] = ws[...]
        out[i, R_W : R_W + FR, F_HID:] = wn[...]


def node_kernel(me, got, y, gp, wg, lhs, rhs, act_all):
    for i in range(NF):
        lhs[i * FR : (i + 1) * FR, :] = got[i, R_W : R_W + FR, :F_HID]
        lhs[F_IN + i * FR : F_IN + (i + 1) * FR, :] = got[i, R_W : R_W + FR, F_HID:]
        rhs[i * FR : (i + 1) * FR, :] = got[i, R_X : R_X + FR, :]
        rhs[F_IN + i * FR : F_IN + (i + 1) * FR, :] = got[i, R_AGG : R_AGG + FR, :]
    tn = (((0,), (0,)), ((), ()))
    pre = lax.dot_general(lhs[...], rhs[...], tn, preferred_element_type=f32)
    gate = 1.0 / (1.0 + jnp.exp(-pre))
    act = pre * gate
    act_all[...] = act
    g = jnp.concatenate([got[i, R_G : R_G + HR, :] for i in range(NF)], axis=0).astype(f32)
    sq = jnp.sum(act * act, axis=0, keepdims=True)
    al = jnp.sum(g * act, axis=0, keepdims=True)
    rs = lax.rsqrt(sq / F_HID + EPS)
    coef = rs * rs * rs * (al / F_HID)
    grad_act = rs * g - act * coef
    grad = (grad_act * gate * (1.0 + pre * (1.0 - gate))).astype(bf16)
    gp[...] = grad
    f = me[0]
    y[...] = (act_all[pl.ds(pl.multiple_of(f * HR, HR), HR), :] * rs).astype(bf16)
    w = lax.dot_general(
        got[f, R_AGG : R_AGG + 2 * FR, :], grad, (((1,), (1,)), ((), ())), preferred_element_type=f32
    ) * (1.0 / math.sqrt(NODES))
    for j in range(8):
        wg[j] = w[j * 8 : (j + 1) * 8, :]


def back_kernel(rows, cols, brows, gp, ws, wn, adj, badj, base, b0, b1, b2, acc, ga):
    own = jnp.dot(ws[...], gp[...], preferred_element_type=f32)
    grad_agg = jnp.dot(wn[...], gp[...], preferred_element_type=f32).astype(bf16)
    for t in range(TILES):
        acc[t] = own[:, t * TILE : (t + 1) * TILE]
        ga[t] = grad_agg[:, t * TILE : (t + 1) * TILE]
    outs = (b0, b1, b2)
    for s in range(ROUNDS * BT):
        b = s % BT
        outs[s // BT][:, b * TILE : (b + 1) * TILE] = jnp.dot(
            ga[brows[s]], badj[s], preferred_element_type=f32
        ).astype(bf16)
    for k in range(KIN):
        acc[cols[k]] += jnp.dot(ga[rows[k]], adj[k], preferred_element_type=f32)
    for t in range(TILES):
        base[:, t * TILE : (t + 1) * TILE] = acc[t]


def join_kernel(send, base, c0, c1, c2, out):
    out[...] = base[...]
    got = (c0, c1, c2)
    for s in range(ROUNDS * BT):
        b = s % BT
        out[:, lanes(send[s])] += got[s // BT][:, b * TILE : (b + 1) * TILE].astype(f32)


def call(kernel, ins, outs, scratch=(), flops=0, nbytes=1 << 20):
    many = isinstance(outs, tuple)
    run = pl.pallas_call(
        kernel,
        out_shape=outs,
        in_specs=[SMEM if i else VMEM for i in ins],
        out_specs=tuple(VMEM for _ in outs) if many else VMEM,
        scratch_shapes=list(scratch),
        cost_estimate=pl.CostEstimate(flops=flops, bytes_accessed=nbytes, transcendentals=0),
    )

    def apply(*args):
        near = [
            a if i else pltpu.with_memory_space_constraint(a, pltpu.VMEM)
            for i, a in zip(ins, args, strict=True)
        ]
        return run(*near)

    return apply


def swap(x, axis):
    return lax.ppermute(x, axis, [(0, 1), (1, 0)])


def shards(x, ws, wn, in_adj, in_rows, in_cols, bnd_adj, bnd_send, bnd_rows, g):
    S = jax.ShapeDtypeStruct
    part = pltpu.VMEM((FR, LOCAL), bf16)
    picked = call(pick_kernel, (1, 0), (part,) * 3)(bnd_send, x)
    got = [swap(picked[r], PAIRS[r]) for r in (2, 1, 0)][::-1]
    give = call(
        agg_kernel,
        (1, 1, 1) + (0,) * 9,
        S((NF, ROWS, LOCAL), bf16),
        (pltpu.VMEM((TILES, FR, TILE), f32),),
    )(in_rows, in_cols, bnd_rows, x, *got, in_adj, bnd_adj, g, ws, wn)
    block = lax.all_to_all(give, "f", 0, 0, tiled=True)
    me = lax.axis_index("f").astype(jnp.int32).reshape(1)
    y, gp, wg = call(
        node_kernel,
        (1, 0),
        (S((HR, LOCAL), bf16), pltpu.VMEM((F_HID, LOCAL), bf16), S((8, 8, F_HID), f32)),
        (
            pltpu.VMEM((2 * F_IN, F_HID), bf16),
            pltpu.VMEM((2 * F_IN, LOCAL), bf16),
            pltpu.VMEM((F_HID, LOCAL), f32),
        ),
    )(me, block)
    wg = lax.all_to_all(wg, Y, 0, 0, tiled=True)
    base, *back = call(
        back_kernel,
        (1, 1, 1) + (0,) * 5,
        (pltpu.VMEM((FR, LOCAL), f32),) + (part,) * 3,
        (pltpu.VMEM((TILES, FR, TILE), f32), pltpu.VMEM((TILES, FR, TILE), bf16)),
    )(in_rows, in_cols, bnd_rows, gp, ws, wn, in_adj, bnd_adj)
    wg, base, *back = lax.optimization_barrier((wg, base, *back))
    home = [None] * ROUNDS
    home[2] = swap(back[2], PAIRS[2])
    wg = jnp.broadcast_to(jnp.sum(wg, axis=0), (16, 8, F_HID))
    wg = lax.all_to_all(wg, ZC, 0, 0, tiled=True)
    home[1] = swap(back[1], PAIRS[1])
    wg, home[2] = lax.optimization_barrier((wg, home[2]))
    wg = jnp.broadcast_to(jnp.sum(wg, axis=0), (8, 8, F_HID))
    wg, back[0] = lax.optimization_barrier((wg, back[0]))
    wg = lax.all_to_all(wg, Y, 0, 0, tiled=True).reshape(2 * FR, F_HID)
    home[0] = swap(back[0], PAIRS[0])
    grad_x = call(join_kernel, (1,) + (0,) * 4, S((FR, LOCAL), f32))(bnd_send, base, *home)
    return y, grad_x, wg[FR:], wg[:FR]


def solution(mesh):
    fine = Mesh(mesh.devices.reshape(SIZES), AXES)
    in_specs = (
        P("f", DOM),
        P("f", None),
        P("f", None),
        P(DOM, None, None),
        P(DOM),
        P(DOM),
        P(DOM, None, None),
        P(DOM),
        P(DOM),
        P("f", DOM),
    )
    out_specs = (P("f", DOM), P("f", DOM), P("f", None), P("f", None))
    return jax.shard_map(shards, mesh=fine, in_specs=in_specs, out_specs=out_specs, check_vma=False)
```

```python
import math

import jax
import jax.numpy as jnp
from jax import lax
from jax.experimental import pallas as pl
from jax.experimental.pallas import tpu as pltpu
from jax.sharding import Mesh
from jax.sharding import PartitionSpec as P

F_IN = 128
F_HID = 256
TILE = 128
TILES = 4
ROUNDS = 3
BT = 4
KIN = 12
NODES = 65536
NF = 4
FR = F_IN // NF
HR = F_HID // NF
LOCAL = TILES * TILE
EPS = 1e-05

AXES = ("y2", "yl", "z2", "z1", "z0", "c", "f")
SIZES = (2, 4, 2, 2, 2, 2, 4)
DOM = AXES[:6]
Y = ("y2", "yl")
NY = 8
ZC = ("z2", "z1", "z0", "c")
NZC = 16
PAIRS = ("z0", "z2", "y2")
FLIP = (2, 8)

R_AGG, R_X, R_G, R_W = 0, FR, 2 * FR, 2 * FR + HR
ROWS = R_W + FR

SMEM = pl.BlockSpec(memory_space=pltpu.SMEM)
VMEM = pl.BlockSpec(memory_space=pltpu.VMEM)
f32, bf16 = jnp.float32, jnp.bfloat16


def lanes(tile):
    return pl.ds(pl.multiple_of(tile * TILE, TILE), TILE)


def tile_of(b):
    return slice(b * TILE, (b + 1) * TILE)


def pick_kernel(send, x, o2, o1, o0):
    for r, out in enumerate((o0, o1, o2)):
        for b in range(BT):
            out[:, tile_of(b)] = x[:, lanes(send[r * BT + b])]


def agg_kernel(rows, cols, brows, x, r2, r1, r0, adj, badj, g, ws, wn, out, acc):
    nt = (((1,), (1,)), ((), ()))
    acc[...] = jnp.zeros_like(acc)
    for k in range(KIN):
        acc[rows[k]] += lax.dot_general(
            x[:, lanes(cols[k])], adj[k], nt, preferred_element_type=f32
        )
    got = (r0, r1, r2)
    for s in range(ROUNDS * BT):
        acc[brows[s]] += lax.dot_general(
            got[s // BT][:, tile_of(s % BT)], badj[s], nt, preferred_element_type=f32
        )
    for i in range(NF):
        for t in range(TILES):
            out[i, R_AGG : R_AGG + FR, tile_of(t)] = acc[t].astype(bf16)
        out[i, R_X : R_X + FR, :] = x[...]
        out[i, R_G : R_G + HR, :] = g[...]
        out[i, R_W : R_W + FR, :F_HID] = ws[...]
        out[i, R_W : R_W + FR, F_HID:] = wn[...]


def split(w):
    high = w.astype(bf16).astype(f32)
    return jnp.concatenate([high, w - high], axis=0).astype(bf16)


def whole(two):
    both = two.astype(f32)
    return both[:8] + both[8:]


def node_kernel(
    me, rows, cols, brows, got, ws, wn, adj, badj, y, base, b2, slots, lhs, rhs, act_all, acc, ga
):
    for i in range(NF):
        lhs[i * FR : (i + 1) * FR, :] = got[i, R_W : R_W + FR, :F_HID]
        lhs[F_IN + i * FR : F_IN + (i + 1) * FR, :] = got[i, R_W : R_W + FR, F_HID:]
        rhs[i * FR : (i + 1) * FR, :] = got[i, R_X : R_X + FR, :]
        rhs[F_IN + i * FR : F_IN + (i + 1) * FR, :] = got[i, R_AGG : R_AGG + FR, :]
    tn = (((0,), (0,)), ((), ()))
    pre = lax.dot_general(lhs[...], rhs[...], tn, preferred_element_type=f32)
    gate = 1.0 / (1.0 + jnp.exp(-pre))
    act = pre * gate
    act_all[...] = act
    g = jnp.concatenate([got[i, R_G : R_G + HR, :] for i in range(NF)], axis=0).astype(f32)
    sq = jnp.sum(act * act, axis=0, keepdims=True)
    al = jnp.sum(g * act, axis=0, keepdims=True)
    rs = lax.rsqrt(sq / F_HID + EPS)
    coef = rs * rs * rs * (al / F_HID)
    grad_act = rs * g - act * coef
    grad = (grad_act * gate * (1.0 + pre * (1.0 - gate))).astype(bf16)
    f = me[0]
    y[...] = (act_all[pl.ds(pl.multiple_of(f * HR, HR), HR), :] * rs).astype(bf16)
    w = lax.dot_general(
        got[f, R_AGG : R_AGG + 2 * FR, :], grad, (((1,), (1,)), ((), ())), preferred_element_type=f32
    ) * (1.0 / math.sqrt(NODES))
    for j in range(NZC):
        slots[j, :16, :] = split(w[j // 2 * 8 : j // 2 * 8 + 8, tile_of(j % 2)])
    own = jnp.dot(ws[...], grad, preferred_element_type=f32)
    grad_agg = jnp.dot(wn[...], grad, preferred_element_type=f32).astype(bf16)
    for t in range(TILES):
        acc[t] = own[:, tile_of(t)]
        ga[t] = grad_agg[:, tile_of(t)]
    for s in range(ROUNDS * BT):
        r, b = divmod(s, BT)
        back = jnp.dot(ga[brows[s]], badj[s], preferred_element_type=f32).astype(bf16)
        if r == 2:
            b2[:, tile_of(b)] = back
        else:
            slots[r * 8 + b, 16:, :] = back[:16]
            slots[r * 8 + 4 + b, 16:, :] = back[16:]
    for k in range(KIN):
        acc[cols[k]] += jnp.dot(ga[rows[k]], adj[k], preferred_element_type=f32)
    for t in range(TILES):
        base[:, tile_of(t)] = acc[t]


def first_sum_kernel(slots, out):
    total = whole(slots[0, :16, :])
    for j in range(1, NZC):
        total += whole(slots[j, :16, :])
    for j in range(NY):
        out[j] = total


def second_sum_kernel(me, terms, slots, out):
    total = terms[0]
    for j in range(1, NY):
        total += terms[j]
    done = split(total)
    flip = jnp.where(me[1] < 8, FLIP[0], FLIP[1])
    for j in range(NZC):
        out[j, :16, :] = done
        out[j, 16:, :] = slots[j ^ flip, 16:, :]


def join_kernel(send, slots, base, c2, gx, gws, gwn):
    for j in range(NZC):
        out, row = (gwn, j // 2 * 8) if j < 8 else (gws, j // 2 * 8 - FR)
        out[row : row + 8, tile_of(j % 2)] = whole(slots[j, :16, :])
    gx[...] = base[...]
    for s in range(ROUNDS * BT):
        r, b = divmod(s, BT)
        if r == 2:
            gx[:, lanes(send[s])] += c2[:, tile_of(b)].astype(f32)
        else:
            gx[:16, lanes(send[s])] += slots[r * 8 + b, 16:, :].astype(f32)
            gx[16:, lanes(send[s])] += slots[r * 8 + 4 + b, 16:, :].astype(f32)


def call(kernel, ins, outs, scratch=(), flops=0, nbytes=1 << 20):
    many = isinstance(outs, tuple)
    run = pl.pallas_call(
        kernel,
        out_shape=outs,
        in_specs=[SMEM if i else VMEM for i in ins],
        out_specs=tuple(VMEM for _ in outs) if many else VMEM,
        scratch_shapes=list(scratch),
        cost_estimate=pl.CostEstimate(flops=flops, bytes_accessed=nbytes, transcendentals=0),
    )

    def apply(*args):
        near = [
            a if i else pltpu.with_memory_space_constraint(a, pltpu.VMEM)
            for i, a in zip(ins, args, strict=True)
        ]
        return run(*near)

    return apply


def swap(x, axis):
    return lax.ppermute(x, axis, [(0, 1), (1, 0)])


def shards(x, ws, wn, in_adj, in_rows, in_cols, bnd_adj, bnd_send, bnd_rows, g):
    S, V = jax.ShapeDtypeStruct, pltpu.VMEM
    part = V((FR, LOCAL), bf16)
    me = jnp.stack([lax.axis_index("f"), lax.axis_index(ZC)]).astype(jnp.int32)
    p2, p1, p0 = call(pick_kernel, (1, 0), (part,) * 3, nbytes=1 << 25)(bnd_send, x)
    got = [swap(p, axis) for p, axis in zip((p2, p1, p0), PAIRS[::-1])]
    give = call(
        agg_kernel,
        (1, 1, 1) + (0,) * 9,
        S((NF, ROWS, LOCAL), bf16),
        (V((TILES, FR, TILE), f32),),
    )(in_rows, in_cols, bnd_rows, x, *got, in_adj, bnd_adj, g, ws, wn)
    block = lax.all_to_all(give, "f", 0, 0, tiled=True)
    y, base, back, slots = call(
        node_kernel,
        (1, 1, 1, 1) + (0,) * 5,
        (S((HR, LOCAL), bf16), V((FR, LOCAL), f32), part, S((NZC, 32, TILE), bf16)),
        (
            V((2 * F_IN, F_HID), bf16),
            V((2 * F_IN, LOCAL), bf16),
            V((F_HID, LOCAL), f32),
            V((TILES, FR, TILE), f32),
            V((TILES, FR, TILE), bf16),
        ),
    )(me, in_rows, in_cols, bnd_rows, block, ws, wn, in_adj, bnd_adj)
    slots = lax.all_to_all(slots, ZC, 0, 0, tiled=True)
    home = swap(back, PAIRS[2])
    terms = call(first_sum_kernel, (0,), S((NY, 8, TILE), f32))(slots)
    terms = lax.all_to_all(terms, Y, 0, 0, tiled=True)
    slots = call(second_sum_kernel, (1, 0, 0), S((NZC, 32, TILE), bf16))(me, terms, slots)
    slots = lax.all_to_all(slots, ZC, 0, 0, tiled=True)
    gx, gws, gwn = call(
        join_kernel,
        (1, 0, 0, 0),
        (S((FR, LOCAL), f32), S((FR, F_HID), f32), S((FR, F_HID), f32)),
    )(bnd_send, slots, base, home)
    return y, gx, gws, gwn


def solution(mesh):
    fine = Mesh(mesh.devices.reshape(SIZES), AXES)
    in_specs = (
        P("f", DOM),
        P("f", None),
        P("f", None),
        P(DOM, None, None),
        P(DOM),
        P(DOM),
        P(DOM, None, None),
        P(DOM),
        P(DOM),
        P("f", DOM),
    )
    out_specs = (P("f", DOM), P("f", DOM), P("f", None), P("f", None))
    return jax.shard_map(shards, mesh=fine, in_specs=in_specs, out_specs=out_specs, check_vma=False)
```

```python
import math

import jax
import jax.numpy as jnp
from jax import lax
from jax.experimental import pallas as pl
from jax.experimental.pallas import tpu as pltpu
from jax.sharding import Mesh
from jax.sharding import PartitionSpec as P

F_IN = 128
F_HID = 256
TILE = 128
TILES = 4
ROUNDS = 3
BT = 4
KIN = 12
NODES = 65536
NF = 4
FR = F_IN // NF
HR = F_HID // NF
LOCAL = TILES * TILE
EPS = 1e-05

AXES = ("y2", "yl", "z2", "z1", "z0", "c", "f")
SIZES = (2, 4, 2, 2, 2, 2, 4)
DOM = AXES[:6]
Y = ("y2", "yl")
NY = 8
ZC = ("z2", "z1", "z0", "c")
NZC = 16
PAIRS = ("z0", "z2", "y2")
FLIP = (2, 8)

R_AGG, R_X, R_G, R_W = 0, FR, 2 * FR, 2 * FR + HR
ROWS = R_W + FR

SMEM = pl.BlockSpec(memory_space=pltpu.SMEM)
VMEM = pl.BlockSpec(memory_space=pltpu.VMEM)
f32, bf16 = jnp.float32, jnp.bfloat16


def lanes(tile):
    return pl.ds(pl.multiple_of(tile * TILE, TILE), TILE)


def tile_of(b):
    return slice(b * TILE, (b + 1) * TILE)


def stage_kernel(send, x, *refs):
    n = (len(refs) - 5) // 2
    far, near, (o2, o1, o0), sem = (x, *refs[:n]), refs[n : 2 * n + 1], refs[2 * n + 1 : -1], refs[-1]
    copies = [
        pltpu.make_async_copy(a, b, sem.at[i]) for i, (a, b) in enumerate(zip(far, near, strict=True))
    ]
    for copy in copies:
        copy.start()
    copies[0].wait()
    for r, out in enumerate((o0, o1, o2)):
        for b in range(BT):
            out[:, tile_of(b)] = near[0][:, lanes(send[r * BT + b])]
    for copy in copies[1:]:
        copy.wait()


def agg_kernel(rows, cols, brows, x, r2, r1, r0, adj, badj, g, ws, wn, out, acc):
    nt = (((1,), (1,)), ((), ()))
    acc[...] = jnp.zeros_like(acc)
    for k in range(KIN):
        acc[rows[k]] += lax.dot_general(
            x[:, lanes(cols[k])], adj[k], nt, preferred_element_type=f32
        )
    got = (r0, r1, r2)
    for s in range(ROUNDS * BT):
        acc[brows[s]] += lax.dot_general(
            got[s // BT][:, tile_of(s % BT)], badj[s], nt, preferred_element_type=f32
        )
    for i in range(NF):
        for t in range(TILES):
            out[i, R_AGG : R_AGG + FR, tile_of(t)] = acc[t].astype(bf16)
        out[i, R_X : R_X + FR, :] = x[...]
        out[i, R_G : R_G + HR, :] = g[...]
        out[i, R_W : R_W + FR, :F_HID] = ws[...]
        out[i, R_W : R_W + FR, F_HID:] = wn[...]


def split(w):
    high = w.astype(bf16).astype(f32)
    return jnp.concatenate([high, w - high], axis=0).astype(bf16)


def whole(two):
    both = two.astype(f32)
    return both[:8] + both[8:]


def node_kernel(
    me, rows, cols, brows, got, ws, wn, adj, badj, y, base, b2, slots, lhs, rhs, act_all, acc, ga
):
    for i in range(NF):
        lhs[i * FR : (i + 1) * FR, :] = got[i, R_W : R_W + FR, :F_HID]
        lhs[F_IN + i * FR : F_IN + (i + 1) * FR, :] = got[i, R_W : R_W + FR, F_HID:]
        rhs[i * FR : (i + 1) * FR, :] = got[i, R_X : R_X + FR, :]
        rhs[F_IN + i * FR : F_IN + (i + 1) * FR, :] = got[i, R_AGG : R_AGG + FR, :]
    tn = (((0,), (0,)), ((), ()))
    pre = lax.dot_general(lhs[...], rhs[...], tn, preferred_element_type=f32)
    gate = 1.0 / (1.0 + jnp.exp(-pre))
    act = pre * gate
    act_all[...] = act
    g = jnp.concatenate([got[i, R_G : R_G + HR, :] for i in range(NF)], axis=0).astype(f32)
    sq = jnp.sum(act * act, axis=0, keepdims=True)
    al = jnp.sum(g * act, axis=0, keepdims=True)
    rs = lax.rsqrt(sq / F_HID + EPS)
    coef = rs * rs * rs * (al / F_HID)
    grad_act = rs * g - act * coef
    grad = (grad_act * gate * (1.0 + pre * (1.0 - gate))).astype(bf16)
    f = me[0]
    y[...] = (act_all[pl.ds(pl.multiple_of(f * HR, HR), HR), :] * rs).astype(bf16)
    w = lax.dot_general(
        got[f, R_AGG : R_AGG + 2 * FR, :], grad, (((1,), (1,)), ((), ())), preferred_element_type=f32
    ) * (1.0 / math.sqrt(NODES))
    for j in range(NZC):
        slots[j, :16, :] = split(w[j // 2 * 8 : j // 2 * 8 + 8, tile_of(j % 2)])
    own = jnp.dot(ws[...], grad, preferred_element_type=f32)
    grad_agg = jnp.dot(wn[...], grad, preferred_element_type=f32).astype(bf16)
    for t in range(TILES):
        acc[t] = own[:, tile_of(t)]
        ga[t] = grad_agg[:, tile_of(t)]
    for s in range(ROUNDS * BT):
        r, b = divmod(s, BT)
        back = jnp.dot(ga[brows[s]], badj[s], preferred_element_type=f32).astype(bf16)
        if r == 2:
            b2[:, tile_of(b)] = back
        else:
            slots[r * 8 + b, 16:, :] = back[:16]
            slots[r * 8 + 4 + b, 16:, :] = back[16:]
    for k in range(KIN):
        acc[cols[k]] += jnp.dot(ga[rows[k]], adj[k], preferred_element_type=f32)
    for t in range(TILES):
        base[:, tile_of(t)] = acc[t]


def first_sum_kernel(slots, out):
    total = whole(slots[0, :16, :])
    for j in range(1, NZC):
        total += whole(slots[j, :16, :])
    for j in range(NY):
        out[j] = total


def second_sum_kernel(me, terms, slots, out):
    total = terms[0]
    for j in range(1, NY):
        total += terms[j]
    done = split(total)
    flip = jnp.where(me[1] < 8, FLIP[0], FLIP[1])
    for j in range(NZC):
        out[j, :16, :] = done
        out[j, 16:, :] = slots[j ^ flip, 16:, :]


def join_kernel(send, slots, base, c2, gx, gws, gwn):
    for j in range(NZC):
        out, row = (gwn, j // 2 * 8) if j < 8 else (gws, j // 2 * 8 - FR)
        out[row : row + 8, tile_of(j % 2)] = whole(slots[j, :16, :])
    gx[...] = base[...]
    for s in range(ROUNDS * BT):
        r, b = divmod(s, BT)
        if r == 2:
            gx[:, lanes(send[s])] += c2[:, tile_of(b)].astype(f32)
        else:
            gx[:16, lanes(send[s])] += slots[r * 8 + b, 16:, :].astype(f32)
            gx[16:, lanes(send[s])] += slots[r * 8 + 4 + b, 16:, :].astype(f32)


def call(kernel, ins, outs, scratch=(), flops=0, nbytes=1 << 20):
    many = isinstance(outs, tuple)
    kinds = (VMEM, SMEM, pl.BlockSpec(memory_space=pl.ANY))
    run = pl.pallas_call(
        kernel,
        out_shape=outs,
        in_specs=[kinds[i] for i in ins],
        out_specs=tuple(VMEM for _ in outs) if many else VMEM,
        scratch_shapes=list(scratch),
        cost_estimate=pl.CostEstimate(flops=flops, bytes_accessed=nbytes, transcendentals=0),
    )

    def apply(*args):
        near = [
            a if i else pltpu.with_memory_space_constraint(a, pltpu.VMEM)
            for i, a in zip(ins, args, strict=True)
        ]
        return run(*near)

    return apply


def swap(x, axis):
    return lax.ppermute(x, axis, [(0, 1), (1, 0)])


def shards(x, ws, wn, in_adj, in_rows, in_cols, bnd_adj, bnd_send, bnd_rows, g):
    S, V = jax.ShapeDtypeStruct, pltpu.VMEM
    part = V((FR, LOCAL), bf16)
    me = jnp.stack([lax.axis_index("f"), lax.axis_index(ZC)]).astype(jnp.int32)
    far = (x, in_adj, bnd_adj, g, ws, wn)
    x, in_adj, bnd_adj, g, ws, wn, p2, p1, p0 = call(
        stage_kernel,
        (1,) + (2,) * len(far),
        tuple(V(a.shape, a.dtype) for a in far) + (part,) * 3,
        (pltpu.SemaphoreType.DMA((len(far),)),),
    )(bnd_send, *far)
    got = [swap(p, axis) for p, axis in zip((p2, p1, p0), PAIRS[::-1])]
    give = call(
        agg_kernel,
        (1, 1, 1) + (0,) * 9,
        V((NF, ROWS, LOCAL), bf16),
        (V((TILES, FR, TILE), f32),),
    )(in_rows, in_cols, bnd_rows, x, *got, in_adj, bnd_adj, g, ws, wn)
    block = lax.all_to_all(give, "f", 0, 0, tiled=True)
    y, base, back, slots = call(
        node_kernel,
        (1, 1, 1, 1) + (0,) * 5,
        (S((HR, LOCAL), bf16), V((FR, LOCAL), f32), part, V((NZC, 32, TILE), bf16)),
        (
            V((2 * F_IN, F_HID), bf16),
            V((2 * F_IN, LOCAL), bf16),
            V((F_HID, LOCAL), f32),
            V((TILES, FR, TILE), f32),
            V((TILES, FR, TILE), bf16),
        ),
    )(me, in_rows, in_cols, bnd_rows, block, ws, wn, in_adj, bnd_adj)
    slots = lax.all_to_all(slots, ZC, 0, 0, tiled=True)
    home = swap(back, PAIRS[2])
    slots, home = lax.optimization_barrier((slots, home))
    terms = call(first_sum_kernel, (0,), V((NY, 8, TILE), f32))(slots)
    terms = lax.all_to_all(terms, Y, 0, 0, tiled=True)
    slots = call(second_sum_kernel, (1, 0, 0), V((NZC, 32, TILE), bf16))(me, terms, slots)
    slots = lax.all_to_all(slots, ZC, 0, 0, tiled=True)
    gx, gws, gwn = call(
        join_kernel,
        (1, 0, 0, 0),
        (S((FR, LOCAL), f32), S((FR, F_HID), f32), S((FR, F_HID), f32)),
    )(bnd_send, slots, base, home)
    return y, gx, gws, gwn


def solution(mesh):
    fine = Mesh(mesh.devices.reshape(SIZES), AXES)
    in_specs = (
        P("f", DOM),
        P("f", None),
        P("f", None),
        P(DOM, None, None),
        P(DOM),
        P(DOM),
        P(DOM, None, None),
        P(DOM),
        P(DOM),
        P("f", DOM),
    )
    out_specs = (P("f", DOM), P("f", DOM), P("f", None), P("f", None))
    return jax.shard_map(shards, mesh=fine, in_specs=in_specs, out_specs=out_specs, check_vma=False)
```

```python
import math

import jax
import jax.numpy as jnp
from jax import lax
from jax.experimental import pallas as pl
from jax.experimental.pallas import tpu as pltpu
from jax.sharding import Mesh
from jax.sharding import PartitionSpec as P

F_IN = 128
F_HID = 256
TILE = 128
TILES = 4
ROUNDS = 3
BT = 4
KIN = 12
NODES = 65536
NF = 4
FR = F_IN // NF
HR = F_HID // NF
LOCAL = TILES * TILE
EPS = 1e-05

AXES = ("y2", "yl", "z2", "z1", "z0", "c", "f")
SIZES = (2, 4, 2, 2, 2, 2, 4)
DOM = AXES[:6]
Y = ("y2", "yl")
NY = 8
ZC = ("z2", "z1", "z0", "c")
NZC = 16
PAIRS = ("z0", "z2", "y2")
FLIP = (2, 8)

R_AGG, R_X, R_G, R_W = 0, FR, 2 * FR, 2 * FR + HR
ROWS = R_W + FR

SMEM = pl.BlockSpec(memory_space=pltpu.SMEM)
VMEM = pl.BlockSpec(memory_space=pltpu.VMEM)
f32, bf16 = jnp.float32, jnp.bfloat16


def lanes(tile):
    return pl.ds(pl.multiple_of(tile * TILE, TILE), TILE)


def tile_of(b):
    return slice(b * TILE, (b + 1) * TILE)


def pick_kernel(send, far, x, o2, o1, o0, sem):
    copy = pltpu.make_async_copy(far, x, sem)
    copy.start()
    copy.wait()
    for r, out in enumerate((o0, o1, o2)):
        for b in range(BT):
            out[:, tile_of(b)] = x[:, lanes(send[r * BT + b])]


NT = (((1,), (1,)), ((), ()))


def inner_kernel(rows, cols, x, *refs):
    far, near, (give, acc, g, sem) = refs[:5], refs[5:9], refs[9:]
    adj, badj, ws, wn = near
    copies = [
        pltpu.make_async_copy(a, b, sem.at[i])
        for i, (a, b) in enumerate(zip(far, (*near, g), strict=True))
    ]
    for copy in copies:
        copy.start()
    acc[...] = jnp.zeros_like(acc)
    for i in range(NF):
        give[i, R_X : R_X + FR, :] = x[...]
    copies[0].wait()
    for k in range(KIN):
        acc[rows[k]] += lax.dot_general(
            x[:, lanes(cols[k])], adj[k], NT, preferred_element_type=f32
        )
    for copy in copies[1:]:
        copy.wait()
    for i in range(NF):
        give[i, R_G : R_G + HR, :] = g[...]
        give[i, R_W : R_W + FR, :F_HID] = ws[...]
        give[i, R_W : R_W + FR, F_HID:] = wn[...]


def outer_kernel(brows, r2, r1, r0, badj, inner, half, give, acc):
    del half
    acc[...] = inner[...]
    got = (r0, r1, r2)
    for s in range(ROUNDS * BT):
        acc[brows[s]] += lax.dot_general(
            got[s // BT][:, tile_of(s % BT)], badj[s], NT, preferred_element_type=f32
        )
    for t in range(TILES):
        part = acc[t].astype(bf16)
        for i in range(NF):
            give[i, R_AGG : R_AGG + FR, tile_of(t)] = part


def split(w):
    high = w.astype(bf16).astype(f32)
    return jnp.concatenate([high, w - high], axis=0).astype(bf16)


def whole(two):
    both = two.astype(f32)
    return both[:8] + both[8:]


def node_kernel(
    rows, cols, brows, got, ws, wn, adj, badj, y, base, b2, slots, lhs, rhs, act_all, acc, ga
):
    for i in range(NF):
        lhs[i * FR : (i + 1) * FR, :] = got[i, R_W : R_W + FR, :F_HID]
        lhs[F_IN + i * FR : F_IN + (i + 1) * FR, :] = got[i, R_W : R_W + FR, F_HID:]
        rhs[i * FR : (i + 1) * FR, :] = got[i, R_X : R_X + FR, :]
        rhs[F_IN + i * FR : F_IN + (i + 1) * FR, :] = got[i, R_AGG : R_AGG + FR, :]
    tn = (((0,), (0,)), ((), ()))
    pre = lax.dot_general(lhs[...], rhs[...], tn, preferred_element_type=f32)
    gate = 1.0 / (1.0 + jnp.exp(-pre))
    act = pre * gate
    act_all[...] = act
    g = jnp.concatenate([got[i, R_G : R_G + HR, :] for i in range(NF)], axis=0).astype(f32)
    sq = jnp.sum(act * act, axis=0, keepdims=True)
    al = jnp.sum(g * act, axis=0, keepdims=True)
    rs = lax.rsqrt(sq / F_HID + EPS)
    coef = rs * rs * rs * (al / F_HID)
    grad_act = rs * g - act * coef
    grad = (grad_act * gate * (1.0 + pre * (1.0 - gate))).astype(bf16)
    f = lax.axis_index("f")
    y[...] = (act_all[pl.ds(pl.multiple_of(f * HR, HR), HR), :] * rs).astype(bf16)
    w = lax.dot_general(
        got[f, R_AGG : R_AGG + 2 * FR, :], grad, (((1,), (1,)), ((), ())), preferred_element_type=f32
    ) * (1.0 / math.sqrt(NODES))
    for j in range(NZC):
        slots[j, :16, :] = split(w[j // 2 * 8 : j // 2 * 8 + 8, tile_of(j % 2)])
    own = jnp.dot(ws[...], grad, preferred_element_type=f32)
    grad_agg = jnp.dot(wn[...], grad, preferred_element_type=f32).astype(bf16)
    for t in range(TILES):
        acc[t] = own[:, tile_of(t)]
        ga[t] = grad_agg[:, tile_of(t)]
    for s in range(ROUNDS * BT):
        r, b = divmod(s, BT)
        back = jnp.dot(ga[brows[s]], badj[s], preferred_element_type=f32).astype(bf16)
        if r == 2:
            b2[:, tile_of(b)] = back
        else:
            slots[r * 8 + b, 16:, :] = back[:16]
            slots[r * 8 + 4 + b, 16:, :] = back[16:]
    for k in range(KIN):
        acc[cols[k]] += jnp.dot(ga[rows[k]], adj[k], preferred_element_type=f32)
    for t in range(TILES):
        base[:, tile_of(t)] = acc[t]


def first_sum_kernel(slots, out):
    total = whole(slots[0, :16, :])
    for j in range(1, NZC):
        total += whole(slots[j, :16, :])
    for j in range(NY):
        out[j] = total


def second_sum_kernel(terms, slots, out):
    total = terms[0]
    for j in range(1, NY):
        total += terms[j]
    done = split(total)
    flip = jnp.where(lax.axis_index("z2") == 0, FLIP[0], FLIP[1])
    for j in range(NZC):
        out[j, :16, :] = done
        out[j, 16:, :] = slots[j ^ flip, 16:, :]


def join_kernel(send, slots, base, c2, gx, gws, gwn):
    for j in range(NZC):
        out, row = (gwn, j // 2 * 8) if j < 8 else (gws, j // 2 * 8 - FR)
        out[row : row + 8, tile_of(j % 2)] = whole(slots[j, :16, :])
    gx[...] = base[...]
    for s in range(ROUNDS * BT):
        r, b = divmod(s, BT)
        if r == 2:
            gx[:, lanes(send[s])] += c2[:, tile_of(b)].astype(f32)
        else:
            gx[:16, lanes(send[s])] += slots[r * 8 + b, 16:, :].astype(f32)
            gx[16:, lanes(send[s])] += slots[r * 8 + 4 + b, 16:, :].astype(f32)


def call(kernel, ins, outs, scratch=(), flops=0, nbytes=1 << 20, aliases=()):
    many = isinstance(outs, tuple)
    kinds = (VMEM, SMEM, pl.BlockSpec(memory_space=pl.ANY))
    run = pl.pallas_call(
        kernel,
        out_shape=outs,
        in_specs=[kinds[i] for i in ins],
        out_specs=tuple(VMEM for _ in outs) if many else VMEM,
        scratch_shapes=list(scratch),
        input_output_aliases=dict(aliases),
        cost_estimate=pl.CostEstimate(flops=flops, bytes_accessed=nbytes, transcendentals=0),
    )

    def apply(*args):
        near = [
            a if i else pltpu.with_memory_space_constraint(a, pltpu.VMEM)
            for i, a in zip(ins, args, strict=True)
        ]
        return run(*near)

    return apply


def swap(x, axis):
    return lax.ppermute(x, axis, [(0, 1), (1, 0)])


def shards(x, ws, wn, in_adj, in_rows, in_cols, bnd_adj, bnd_send, bnd_rows, g):
    S, V = jax.ShapeDtypeStruct, pltpu.VMEM
    part = V((FR, LOCAL), bf16)
    sems = pltpu.SemaphoreType.DMA
    here, p2, p1, p0 = call(pick_kernel, (1, 2), (part,) * 4, (sems(()),))(bnd_send, x)
    got = [swap(p, axis) for p, axis in zip((p2, p1, p0), PAIRS[::-1])]
    far = (in_adj, bnd_adj, ws, wn)
    in_adj, bnd_adj, ws, wn, give, acc = call(
        inner_kernel,
        (1, 1, 0) + (2,) * 5,
        tuple(V(a.shape, a.dtype) for a in far)
        + (V((NF, ROWS, LOCAL), bf16), V((TILES, FR, TILE), f32)),
        (V((HR, LOCAL), bf16), sems((5,))),
    )(in_rows, in_cols, here, *far, g)
    give = call(
        outer_kernel,
        (1,) + (0,) * 6,
        V((NF, ROWS, LOCAL), bf16),
        (V((TILES, FR, TILE), f32),),
        aliases=((6, 0),),
    )(bnd_rows, *got, bnd_adj, acc, give)
    block = lax.all_to_all(give, "f", 0, 0, tiled=True)
    y, base, back, slots = call(
        node_kernel,
        (1, 1, 1) + (0,) * 5,
        (V((HR, LOCAL), bf16), V((FR, LOCAL), f32), part, V((NZC, 32, TILE), bf16)),
        (
            V((2 * F_IN, F_HID), bf16),
            V((2 * F_IN, LOCAL), bf16),
            V((F_HID, LOCAL), f32),
            V((TILES, FR, TILE), f32),
            V((TILES, FR, TILE), bf16),
        ),
    )(in_rows, in_cols, bnd_rows, block, ws, wn, in_adj, bnd_adj)
    slots = lax.all_to_all(slots, ZC, 0, 0, tiled=True)
    home = swap(back, PAIRS[2])
    slots, home = lax.optimization_barrier((slots, home))
    terms = call(first_sum_kernel, (0,), V((NY, 8, TILE), f32))(slots)
    terms = lax.all_to_all(terms, Y, 0, 0, tiled=True)
    slots = call(second_sum_kernel, (0, 0), V((NZC, 32, TILE), bf16))(terms, slots)
    slots = lax.all_to_all(slots, ZC, 0, 0, tiled=True)
    gx, gws, gwn = call(
        join_kernel,
        (1, 0, 0, 0),
        (S((FR, LOCAL), f32), S((FR, F_HID), f32), S((FR, F_HID), f32)),
    )(bnd_send, slots, base, home)
    return y, gx, gws, gwn


def solution(mesh):
    fine = Mesh(mesh.devices.reshape(SIZES), AXES)
    in_specs = (
        P("f", DOM),
        P("f", None),
        P("f", None),
        P(DOM, None, None),
        P(DOM),
        P(DOM),
        P(DOM, None, None),
        P(DOM),
        P(DOM),
        P("f", DOM),
    )
    out_specs = (P("f", DOM), P("f", DOM), P("f", None), P("f", None))
    return jax.shard_map(shards, mesh=fine, in_specs=in_specs, out_specs=out_specs, check_vma=False)
```

```python
import math

import jax
import jax.numpy as jnp
from jax import lax
from jax.experimental import pallas as pl
from jax.experimental.pallas import tpu as pltpu
from jax.sharding import Mesh
from jax.sharding import PartitionSpec as P

F_IN = 128
F_HID = 256
TILE = 128
TILES = 4
ROUNDS = 3
BT = 4
KIN = 12
NODES = 65536
NF = 4
FR = F_IN // NF
HR = F_HID // NF
LOCAL = TILES * TILE
EPS = 1e-05

AXES = ("y2", "yl", "z2", "z1", "z0", "c", "f")
SIZES = (2, 4, 2, 2, 2, 2, 4)
DOM = AXES[:6]
Y = ("y2", "yl")
NY = 8
ZC = ("z2", "z1", "z0", "c")
NZC = 16
PAIRS = ("z0", "z2", "y2")
FLIP = (2, 8)

R_AGG, R_X, R_G, R_W = 0, FR, 2 * FR, 2 * FR + HR
ROWS = R_W + FR

SMEM = pl.BlockSpec(memory_space=pltpu.SMEM)
VMEM = pl.BlockSpec(memory_space=pltpu.VMEM)
f32, bf16 = jnp.float32, jnp.bfloat16


def lanes(tile):
    return pl.ds(pl.multiple_of(tile * TILE, TILE), TILE)


def tile_of(b):
    return slice(b * TILE, (b + 1) * TILE)


def pick_kernel(send, x, here, o2, o1, o0):
    here[...] = x[...]
    for r, out in enumerate((o0, o1, o2)):
        for b in range(BT):
            out[:, tile_of(b)] = x[:, lanes(send[r * BT + b])]


NT = (((1,), (1,)), ((), ()))


def inner_kernel(rows, cols, x, *refs):
    far, near, (give, acc, g, sem) = refs[:5], refs[5:9], refs[9:]
    adj, badj, ws, wn = near
    copies = [
        pltpu.make_async_copy(a, b, sem.at[i])
        for i, (a, b) in enumerate(zip(far, (*near, g), strict=True))
    ]
    for copy in copies:
        copy.start()
    acc[...] = jnp.zeros_like(acc)
    for i in range(NF):
        give[i, R_X : R_X + FR, :] = x[...]
    copies[0].wait()
    for k in range(KIN):
        acc[rows[k]] += lax.dot_general(
            x[:, lanes(cols[k])], adj[k], NT, preferred_element_type=f32
        )
    for copy in copies[1:]:
        copy.wait()
    for i in range(NF):
        give[i, R_G : R_G + HR, :] = g[...]
        give[i, R_W : R_W + FR, :F_HID] = ws[...]
        give[i, R_W : R_W + FR, F_HID:] = wn[...]


def outer_kernel(brows, r2, r1, r0, badj, inner, half, give, acc):
    del half
    acc[...] = inner[...]
    got = (r0, r1, r2)
    for s in range(ROUNDS * BT):
        acc[brows[s]] += lax.dot_general(
            got[s // BT][:, tile_of(s % BT)], badj[s], NT, preferred_element_type=f32
        )
    for t in range(TILES):
        part = acc[t].astype(bf16)
        for i in range(NF):
            give[i, R_AGG : R_AGG + FR, tile_of(t)] = part


def split(w):
    high = w.astype(bf16).astype(f32)
    return jnp.concatenate([high, w - high], axis=0).astype(bf16)


def whole(two):
    both = two.astype(f32)
    return both[:8] + both[8:]


def node_kernel(brows, got, ws, wn, badj, y, acc, ga, b2, slots, lhs, rhs, act_all):
    for i in range(NF):
        lhs[i * FR : (i + 1) * FR, :] = got[i, R_W : R_W + FR, :F_HID]
        lhs[F_IN + i * FR : F_IN + (i + 1) * FR, :] = got[i, R_W : R_W + FR, F_HID:]
        rhs[i * FR : (i + 1) * FR, :] = got[i, R_X : R_X + FR, :]
        rhs[F_IN + i * FR : F_IN + (i + 1) * FR, :] = got[i, R_AGG : R_AGG + FR, :]
    tn = (((0,), (0,)), ((), ()))
    pre = lax.dot_general(lhs[...], rhs[...], tn, preferred_element_type=f32)
    gate = 1.0 / (1.0 + jnp.exp(-pre))
    act = pre * gate
    act_all[...] = act
    g = jnp.concatenate([got[i, R_G : R_G + HR, :] for i in range(NF)], axis=0).astype(f32)
    sq = jnp.sum(act * act, axis=0, keepdims=True)
    al = jnp.sum(g * act, axis=0, keepdims=True)
    rs = lax.rsqrt(sq / F_HID + EPS)
    coef = rs * rs * rs * (al / F_HID)
    grad_act = rs * g - act * coef
    grad = (grad_act * gate * (1.0 + pre * (1.0 - gate))).astype(bf16)
    f = lax.axis_index("f")
    y[...] = (act_all[pl.ds(pl.multiple_of(f * HR, HR), HR), :] * rs).astype(bf16)
    w = lax.dot_general(
        got[f, R_AGG : R_AGG + 2 * FR, :], grad, (((1,), (1,)), ((), ())), preferred_element_type=f32
    ) * (1.0 / math.sqrt(NODES))
    for j in range(NZC):
        slots[j, :16, :] = split(w[j // 2 * 8 : j // 2 * 8 + 8, tile_of(j % 2)])
    both = jnp.dot(
        jnp.concatenate([ws[...], wn[...]], axis=0), grad, preferred_element_type=f32
    )
    for t in range(TILES):
        acc[t] = both[:FR, tile_of(t)]
        ga[t] = both[FR:, tile_of(t)].astype(bf16)
    for s in range(ROUNDS * BT):
        r, b = divmod(s, BT)
        back = jnp.dot(ga[brows[s]], badj[s], preferred_element_type=f32).astype(bf16)
        if r == 2:
            b2[:, tile_of(b)] = back
        else:
            slots[r * 8 + b, 16:, :] = back[:16]
            slots[r * 8 + 4 + b, 16:, :] = back[16:]


def back_kernel(rows, cols, own, ga, adj, y, base, out, acc):
    out[...] = y[...]
    acc[...] = own[...]
    for k in range(KIN):
        acc[cols[k]] += jnp.dot(ga[rows[k]], adj[k], preferred_element_type=f32)
    for t in range(TILES):
        base[:, tile_of(t)] = acc[t]


def first_sum_kernel(slots, out):
    total = whole(slots[0, :16, :])
    for j in range(1, NZC):
        total += whole(slots[j, :16, :])
    for j in range(NY):
        out[j] = total


def second_sum_kernel(terms, slots, out):
    total = terms[0]
    for j in range(1, NY):
        total += terms[j]
    done = split(total)
    flip = jnp.where(lax.axis_index("z2") == 0, FLIP[0], FLIP[1])
    for j in range(NZC):
        out[j, :16, :] = done
        out[j, 16:, :] = slots[j ^ flip, 16:, :]


def join_kernel(send, slots, base, c2, gx, gws, gwn):
    for j in range(NZC):
        out, row = (gwn, j // 2 * 8) if j < 8 else (gws, j // 2 * 8 - FR)
        out[row : row + 8, tile_of(j % 2)] = whole(slots[j, :16, :])
    gx[...] = base[...]
    for s in range(ROUNDS * BT):
        r, b = divmod(s, BT)
        if r == 2:
            gx[:, lanes(send[s])] += c2[:, tile_of(b)].astype(f32)
        else:
            gx[:16, lanes(send[s])] += slots[r * 8 + b, 16:, :].astype(f32)
            gx[16:, lanes(send[s])] += slots[r * 8 + 4 + b, 16:, :].astype(f32)


def call(kernel, ins, outs, scratch=(), flops=0, nbytes=1 << 20, aliases=()):
    many = isinstance(outs, tuple)
    kinds = (VMEM, SMEM, pl.BlockSpec(memory_space=pl.ANY), VMEM)
    run = pl.pallas_call(
        kernel,
        out_shape=outs,
        in_specs=[kinds[i] for i in ins],
        out_specs=tuple(VMEM for _ in outs) if many else VMEM,
        scratch_shapes=list(scratch),
        input_output_aliases=dict(aliases),
        cost_estimate=pl.CostEstimate(flops=flops, bytes_accessed=nbytes, transcendentals=0),
    )

    def apply(*args):
        near = [
            a if i else pltpu.with_memory_space_constraint(a, pltpu.VMEM)
            for i, a in zip(ins, args, strict=True)
        ]
        return run(*near)

    return apply


def swap(x, axis):
    return lax.ppermute(x, axis, [(0, 1), (1, 0)])


def shards(x, ws, wn, in_adj, in_rows, in_cols, bnd_adj, bnd_send, bnd_rows, g):
    S, V = jax.ShapeDtypeStruct, pltpu.VMEM
    part = V((FR, LOCAL), bf16)
    sems = pltpu.SemaphoreType.DMA
    here, p2, p1, p0 = call(pick_kernel, (1, 3), (part,) * 4)(bnd_send, x)
    got = [swap(p, axis) for p, axis in zip((p2, p1, p0), PAIRS[::-1])]
    far = (in_adj, bnd_adj, ws, wn)
    in_adj, bnd_adj, ws, wn, give, acc = call(
        inner_kernel,
        (1, 1, 0) + (2,) * 5,
        tuple(V(a.shape, a.dtype) for a in far)
        + (V((NF, ROWS, LOCAL), bf16), V((TILES, FR, TILE), f32)),
        (V((HR, LOCAL), bf16), sems((5,))),
    )(in_rows, in_cols, here, *far, g)
    give = call(
        outer_kernel,
        (1,) + (0,) * 6,
        V((NF, ROWS, LOCAL), bf16),
        (V((TILES, FR, TILE), f32),),
        aliases=((6, 0),),
    )(bnd_rows, *got, bnd_adj, acc, give)
    block = lax.all_to_all(give, "f", 0, 0, tiled=True)
    y, own, ga, back, slots = call(
        node_kernel,
        (1,) + (0,) * 4,
        (
            V((HR, LOCAL), bf16),
            V((TILES, FR, TILE), f32),
            V((TILES, FR, TILE), bf16),
            part,
            S((NZC, 32, TILE), bf16),
        ),
        (V((2 * F_IN, F_HID), bf16), V((2 * F_IN, LOCAL), bf16), V((F_HID, LOCAL), f32)),
    )(bnd_rows, block, ws, wn, bnd_adj)
    slots = lax.all_to_all(slots, ZC, 0, 0, tiled=True)
    home = swap(back, PAIRS[2])
    base, y = call(
        back_kernel,
        (1, 1) + (0,) * 4,
        (V((FR, LOCAL), f32), S((HR, LOCAL), bf16)),
        (V((TILES, FR, TILE), f32),),
    )(in_rows, in_cols, own, ga, in_adj, y)
    slots, home, base = lax.optimization_barrier((slots, home, base))
    terms = call(first_sum_kernel, (0,), V((NY, 8, TILE), f32))(slots)
    terms = lax.all_to_all(terms, Y, 0, 0, tiled=True)
    slots = call(second_sum_kernel, (0, 0), V((NZC, 32, TILE), bf16))(terms, slots)
    slots = lax.all_to_all(slots, ZC, 0, 0, tiled=True)
    gx, gws, gwn = call(
        join_kernel,
        (1, 0, 0, 0),
        (S((FR, LOCAL), f32), S((FR, F_HID), f32), S((FR, F_HID), f32)),
    )(bnd_send, slots, base, home)
    return y, gx, gws, gwn


def solution(mesh):
    fine = Mesh(mesh.devices.reshape(SIZES), AXES)
    in_specs = (
        P("f", DOM),
        P("f", None),
        P("f", None),
        P(DOM, None, None),
        P(DOM),
        P(DOM),
        P(DOM, None, None),
        P(DOM),
        P(DOM),
        P("f", DOM),
    )
    out_specs = (P("f", DOM), P("f", DOM), P("f", None), P("f", None))
    return jax.shard_map(shards, mesh=fine, in_specs=in_specs, out_specs=out_specs, check_vma=False)
```

```python
import math

import jax
import jax.numpy as jnp
from jax import lax
from jax.experimental import pallas as pl
from jax.experimental.pallas import tpu as pltpu
from jax.sharding import Mesh
from jax.sharding import PartitionSpec as P

F_IN = 128
F_HID = 256
TILE = 128
TILES = 4
ROUNDS = 3
BT = 4
KIN = 12
NODES = 65536
NF = 4
FR = F_IN // NF
HR = F_HID // NF
LOCAL = TILES * TILE
EPS = 1e-05

AXES = ("y2", "yl", "z2", "z1", "z0", "c", "f")
SIZES = (2, 4, 2, 2, 2, 2, 4)
DOM = AXES[:6]
Y = ("y2", "yl")
NY = 8
ZC = ("z2", "z1", "z0", "c")
NZC = 16
PAIRS = ("z0", "z2", "y2")
FLIP = (2, 8)

R_AGG, R_X, R_G, R_W = 0, FR, 2 * FR, 2 * FR + HR
ROWS = R_W + FR

SMEM = pl.BlockSpec(memory_space=pltpu.SMEM)
VMEM = pl.BlockSpec(memory_space=pltpu.VMEM)
f32, bf16 = jnp.float32, jnp.bfloat16


def lanes(tile):
    return pl.ds(pl.multiple_of(tile * TILE, TILE), TILE)


def tile_of(b):
    return slice(b * TILE, (b + 1) * TILE)


def pick_kernel(send, x, here, o2, o1, o0):
    here[...] = x[...]
    for r, out in enumerate((o0, o1, o2)):
        for b in range(BT):
            out[:, tile_of(b)] = x[:, lanes(send[r * BT + b])]


NT = (((1,), (1,)), ((), ()))


def inner_kernel(rows, cols, x, *refs):
    far, near, (give, acc, g, sem) = refs[:5], refs[5:9], refs[9:]
    adj, badj, ws, wn = near
    copies = [
        pltpu.make_async_copy(a, b, sem.at[i])
        for i, (a, b) in enumerate(zip(far, (*near, g), strict=True))
    ]
    for copy in copies:
        copy.start()
    acc[...] = jnp.zeros_like(acc)
    for i in range(NF):
        give[i, R_X : R_X + FR, :] = x[...]
    copies[0].wait()
    for k in range(KIN):
        acc[rows[k]] += lax.dot_general(
            x[:, lanes(cols[k])], adj[k], NT, preferred_element_type=f32
        )
    for copy in copies[1:]:
        copy.wait()
    for i in range(NF):
        give[i, R_G : R_G + HR, :] = g[...]
        give[i, R_W : R_W + FR, :F_HID] = ws[...]
        give[i, R_W : R_W + FR, F_HID:] = wn[...]


def outer_kernel(brows, r2, r1, r0, badj, inner, half, give, acc):
    del half
    acc[...] = inner[...]
    got = (r0, r1, r2)
    for s in range(ROUNDS * BT):
        acc[brows[s]] += lax.dot_general(
            got[s // BT][:, tile_of(s % BT)], badj[s], NT, preferred_element_type=f32
        )
    for t in range(TILES):
        part = acc[t].astype(bf16)
        for i in range(NF):
            give[i, R_AGG : R_AGG + FR, tile_of(t)] = part


def split(w):
    high = w.astype(bf16).astype(f32)
    return jnp.concatenate([high, w - high], axis=0).astype(bf16)


def whole(two):
    both = two.astype(f32)
    return both[:8] + both[8:]


def node_kernel(brows, got, ws, wn, badj, y, acc, ga, b2, slots, lhs, rhs, act_all):
    for i in range(NF):
        lhs[i * FR : (i + 1) * FR, :] = got[i, R_W : R_W + FR, :F_HID]
        lhs[F_IN + i * FR : F_IN + (i + 1) * FR, :] = got[i, R_W : R_W + FR, F_HID:]
        rhs[i * FR : (i + 1) * FR, :] = got[i, R_X : R_X + FR, :]
        rhs[F_IN + i * FR : F_IN + (i + 1) * FR, :] = got[i, R_AGG : R_AGG + FR, :]
    tn = (((0,), (0,)), ((), ()))
    pre = lax.dot_general(lhs[...], rhs[...], tn, preferred_element_type=f32)
    gate = 1.0 / (1.0 + jnp.exp(-pre))
    act = pre * gate
    act_all[...] = act
    g = jnp.concatenate([got[i, R_G : R_G + HR, :] for i in range(NF)], axis=0).astype(f32)
    sq = jnp.sum(act * act, axis=0, keepdims=True)
    al = jnp.sum(g * act, axis=0, keepdims=True)
    rs = lax.rsqrt(sq / F_HID + EPS)
    coef = rs * rs * rs * (al / F_HID)
    grad_act = rs * g - act * coef
    grad = (grad_act * gate * (1.0 + pre * (1.0 - gate))).astype(bf16)
    f = lax.axis_index("f")
    y[...] = (act_all[pl.ds(pl.multiple_of(f * HR, HR), HR), :] * rs).astype(bf16)
    w = lax.dot_general(
        got[f, R_AGG : R_AGG + 2 * FR, :], grad, (((1,), (1,)), ((), ())), preferred_element_type=f32
    ) * (1.0 / math.sqrt(NODES))
    for j in range(NZC):
        slots[j, :16, :] = split(w[j // 2 * 8 : j // 2 * 8 + 8, tile_of(j % 2)])
    both = jnp.dot(
        jnp.concatenate([ws[...], wn[...]], axis=0), grad, preferred_element_type=f32
    )
    for t in range(TILES):
        acc[t] = both[:FR, tile_of(t)]
        ga[t] = both[FR:, tile_of(t)].astype(bf16)
    for s in range(ROUNDS * BT):
        r, b = divmod(s, BT)
        back = jnp.dot(ga[brows[s]], badj[s], preferred_element_type=f32)
        if r == 2:
            b2[:, tile_of(b)] = back
        else:
            back = back.astype(bf16)
            slots[r * 8 + b, 16:, :] = back[:16]
            slots[r * 8 + 4 + b, 16:, :] = back[16:]


def back_kernel(rows, cols, own, ga, adj, y, base, out, acc):
    out[...] = y[...]
    acc[...] = own[...]
    for k in range(KIN):
        acc[cols[k]] += jnp.dot(ga[rows[k]], adj[k], preferred_element_type=f32)
    for t in range(TILES):
        base[:, tile_of(t)] = acc[t]


def first_sum_kernel(slots, out):
    total = whole(slots[0, :16, :])
    for j in range(1, NZC):
        total += whole(slots[j, :16, :])
    for j in range(NY):
        out[j] = total


def second_sum_kernel(terms, slots, out):
    total = terms[0]
    for j in range(1, NY):
        total += terms[j]
    done = split(total)
    flip = jnp.where(lax.axis_index("z2") == 0, FLIP[0], FLIP[1])
    for j in range(NZC):
        out[j, :16, :] = done
        out[j, 16:, :] = slots[j ^ flip, 16:, :]


def join_kernel(send, slots, base, c2, gx, gws, gwn):
    for j in range(NZC):
        out, row = (gwn, j // 2 * 8) if j < 8 else (gws, j // 2 * 8 - FR)
        out[row : row + 8, tile_of(j % 2)] = whole(slots[j, :16, :])
    gx[...] = base[...]
    for s in range(ROUNDS * BT):
        r, b = divmod(s, BT)
        if r == 2:
            gx[:, lanes(send[s])] += c2[:, tile_of(b)]
        else:
            gx[:16, lanes(send[s])] += slots[r * 8 + b, 16:, :].astype(f32)
            gx[16:, lanes(send[s])] += slots[r * 8 + 4 + b, 16:, :].astype(f32)


def call(kernel, ins, outs, scratch=(), flops=0, nbytes=1 << 20, aliases=()):
    many = isinstance(outs, tuple)
    kinds = (VMEM, SMEM, pl.BlockSpec(memory_space=pl.ANY), VMEM)
    run = pl.pallas_call(
        kernel,
        out_shape=outs,
        in_specs=[kinds[i] for i in ins],
        out_specs=tuple(VMEM for _ in outs) if many else VMEM,
        scratch_shapes=list(scratch),
        input_output_aliases=dict(aliases),
        cost_estimate=pl.CostEstimate(flops=flops, bytes_accessed=nbytes, transcendentals=0),
    )

    def apply(*args):
        near = [
            a if i else pltpu.with_memory_space_constraint(a, pltpu.VMEM)
            for i, a in zip(ins, args, strict=True)
        ]
        return run(*near)

    return apply


def swap(x, axis):
    return lax.ppermute(x, axis, [(0, 1), (1, 0)])


def shards(x, ws, wn, in_adj, in_rows, in_cols, bnd_adj, bnd_send, bnd_rows, g):
    S, V = jax.ShapeDtypeStruct, pltpu.VMEM
    part = V((FR, LOCAL), bf16)
    sems = pltpu.SemaphoreType.DMA
    here, p2, p1, p0 = call(pick_kernel, (1, 3), (part,) * 4)(bnd_send, x)
    got = [swap(p, axis) for p, axis in zip((p2, p1, p0), PAIRS[::-1])]
    far = (in_adj, bnd_adj, ws, wn)
    in_adj, bnd_adj, ws, wn, give, acc = call(
        inner_kernel,
        (1, 1, 0) + (2,) * 5,
        tuple(V(a.shape, a.dtype) for a in far)
        + (V((NF, ROWS, LOCAL), bf16), V((TILES, FR, TILE), f32)),
        (V((HR, LOCAL), bf16), sems((5,))),
    )(in_rows, in_cols, here, *far, g)
    give = call(
        outer_kernel,
        (1,) + (0,) * 6,
        V((NF, ROWS, LOCAL), bf16),
        (V((TILES, FR, TILE), f32),),
        aliases=((6, 0),),
    )(bnd_rows, *got, bnd_adj, acc, give)
    block = lax.all_to_all(give, "f", 0, 0, tiled=True)
    y, own, ga, back, slots = call(
        node_kernel,
        (1,) + (0,) * 4,
        (
            V((HR, LOCAL), bf16),
            V((TILES, FR, TILE), f32),
            V((TILES, FR, TILE), bf16),
            V((FR, LOCAL), f32),
            S((NZC, 32, TILE), bf16),
        ),
        (V((2 * F_IN, F_HID), bf16), V((2 * F_IN, LOCAL), bf16), V((F_HID, LOCAL), f32)),
    )(bnd_rows, block, ws, wn, bnd_adj)
    slots = lax.all_to_all(slots, ZC, 0, 0, tiled=True)
    home = swap(back, PAIRS[2])
    base, y = call(
        back_kernel,
        (1, 1) + (0,) * 4,
        (V((FR, LOCAL), f32), S((HR, LOCAL), bf16)),
        (V((TILES, FR, TILE), f32),),
    )(in_rows, in_cols, own, ga, in_adj, y)
    slots, base = lax.optimization_barrier((slots, base))
    terms = call(first_sum_kernel, (0,), V((NY, 8, TILE), f32))(slots)
    terms = lax.all_to_all(terms, Y, 0, 0, tiled=True)
    terms, home = lax.optimization_barrier((terms, home))
    slots = call(second_sum_kernel, (0, 0), V((NZC, 32, TILE), bf16))(terms, slots)
    slots = lax.all_to_all(slots, ZC, 0, 0, tiled=True)
    gx, gws, gwn = call(
        join_kernel,
        (1, 0, 0, 0),
        (S((FR, LOCAL), f32), S((FR, F_HID), f32), S((FR, F_HID), f32)),
    )(bnd_send, slots, base, home)
    return y, gx, gws, gwn


def solution(mesh):
    fine = Mesh(mesh.devices.reshape(SIZES), AXES)
    in_specs = (
        P("f", DOM),
        P("f", None),
        P("f", None),
        P(DOM, None, None),
        P(DOM),
        P(DOM),
        P(DOM, None, None),
        P(DOM),
        P(DOM),
        P("f", DOM),
    )
    out_specs = (P("f", DOM), P("f", DOM), P("f", None), P("f", None))
    return jax.shard_map(shards, mesh=fine, in_specs=in_specs, out_specs=out_specs, check_vma=False)
```

```python
import math

import jax
import jax.numpy as jnp
from jax import lax
from jax.experimental import pallas as pl
from jax.experimental.pallas import tpu as pltpu
from jax.sharding import Mesh
from jax.sharding import PartitionSpec as P

F_IN = 128
F_HID = 256
TILE = 128
TILES = 4
ROUNDS = 3
BT = 4
KIN = 12
NODES = 65536
NF = 4
FR = F_IN // NF
HR = F_HID // NF
LOCAL = TILES * TILE
EPS = 1e-05

AXES = ("y2", "yl", "z2", "z1", "z0", "c", "f")
SIZES = (2, 4, 2, 2, 2, 2, 4)
DOM = AXES[:6]
Y = ("y2", "yl")
NY = 8
ZC = ("z2", "z1", "z0", "c")
NZC = 16
PAIRS = ("z0", "z2", "y2")

R_AGG, R_X, R_G, R_W = 0, FR, 2 * FR, 2 * FR + HR
ROWS = R_W + FR

SMEM = pl.BlockSpec(memory_space=pltpu.SMEM)
VMEM = pl.BlockSpec(memory_space=pltpu.VMEM)
f32, bf16 = jnp.float32, jnp.bfloat16


def lanes(tile):
    return pl.ds(pl.multiple_of(tile * TILE, TILE), TILE)


def tile_of(b):
    return slice(b * TILE, (b + 1) * TILE)


def pick_kernel(send, x, here, o2, o1, o0):
    here[...] = x[...]
    for r, out in enumerate((o0, o1, o2)):
        for b in range(BT):
            out[:, tile_of(b)] = x[:, lanes(send[r * BT + b])]


NT = (((1,), (1,)), ((), ()))


def inner_kernel(rows, cols, x, *refs):
    far, near, (give, acc, g, sem) = refs[:5], refs[5:9], refs[9:]
    adj, badj, ws, wn = near
    copies = [
        pltpu.make_async_copy(a, b, sem.at[i])
        for i, (a, b) in enumerate(zip(far, (*near, g), strict=True))
    ]
    for copy in copies:
        copy.start()
    acc[...] = jnp.zeros_like(acc)
    for i in range(NF):
        give[i, R_X : R_X + FR, :] = x[...]
    copies[0].wait()
    for k in range(KIN):
        acc[rows[k]] += lax.dot_general(
            x[:, lanes(cols[k])], adj[k], NT, preferred_element_type=f32
        )
    for copy in copies[1:]:
        copy.wait()
    for i in range(NF):
        give[i, R_G : R_G + HR, :] = g[...]
        give[i, R_W : R_W + FR, :F_HID] = ws[...]
        give[i, R_W : R_W + FR, F_HID:] = wn[...]


def outer_kernel(brows, r2, r1, r0, badj, inner, half, give, acc):
    del half
    acc[...] = inner[...]
    got = (r0, r1, r2)
    for s in range(ROUNDS * BT):
        acc[brows[s]] += lax.dot_general(
            got[s // BT][:, tile_of(s % BT)], badj[s], NT, preferred_element_type=f32
        )
    for t in range(TILES):
        part = acc[t].astype(bf16)
        for i in range(NF):
            give[i, R_AGG : R_AGG + FR, tile_of(t)] = part


def node_kernel(brows, got, ws, wn, badj, y, acc, ga, b0, b1, b2, slots, lhs, rhs, act_all):
    for i in range(NF):
        lhs[i * FR : (i + 1) * FR, :] = got[i, R_W : R_W + FR, :F_HID]
        lhs[F_IN + i * FR : F_IN + (i + 1) * FR, :] = got[i, R_W : R_W + FR, F_HID:]
        rhs[i * FR : (i + 1) * FR, :] = got[i, R_X : R_X + FR, :]
        rhs[F_IN + i * FR : F_IN + (i + 1) * FR, :] = got[i, R_AGG : R_AGG + FR, :]
    tn = (((0,), (0,)), ((), ()))
    pre = lax.dot_general(lhs[...], rhs[...], tn, preferred_element_type=f32)
    gate = 1.0 / (1.0 + jnp.exp(-pre))
    act = pre * gate
    act_all[...] = act
    g = jnp.concatenate([got[i, R_G : R_G + HR, :] for i in range(NF)], axis=0).astype(f32)
    sq = jnp.sum(act * act, axis=0, keepdims=True)
    al = jnp.sum(g * act, axis=0, keepdims=True)
    rs = lax.rsqrt(sq / F_HID + EPS)
    coef = rs * rs * rs * (al / F_HID)
    grad_act = rs * g - act * coef
    grad = (grad_act * gate * (1.0 + pre * (1.0 - gate))).astype(bf16)
    f = lax.axis_index("f")
    y[...] = (act_all[pl.ds(pl.multiple_of(f * HR, HR), HR), :] * rs).astype(bf16)
    w = lax.dot_general(
        got[f, R_AGG : R_AGG + 2 * FR, :], grad, (((1,), (1,)), ((), ())), preferred_element_type=f32
    ) * (1.0 / math.sqrt(NODES))
    for j in range(NZC):
        slots[j] = w[j // 2 * 8 : j // 2 * 8 + 8, tile_of(j % 2)]
    both = jnp.dot(
        jnp.concatenate([ws[...], wn[...]], axis=0), grad, preferred_element_type=f32
    )
    for t in range(TILES):
        acc[t] = both[:FR, tile_of(t)]
        ga[t] = both[FR:, tile_of(t)].astype(bf16)
    outs = (b0, b1, b2)
    for s in range(ROUNDS * BT):
        r, b = divmod(s, BT)
        outs[r][:, tile_of(b)] = jnp.dot(
            ga[brows[s]], badj[s], preferred_element_type=f32
        ).astype(outs[r].dtype)


def back_kernel(rows, cols, own, ga, adj, y, base, out, acc):
    out[...] = y[...]
    acc[...] = own[...]
    for k in range(KIN):
        acc[cols[k]] += jnp.dot(ga[rows[k]], adj[k], preferred_element_type=f32)
    for t in range(TILES):
        base[:, tile_of(t)] = acc[t]


def sum_kernel(terms, out):
    total = terms[0]
    for j in range(1, terms.shape[0]):
        total += terms[j]
    for j in range(out.shape[0]):
        out[j] = total.astype(out.dtype)


def grad_x_kernel(send, base, c0, c1, c2, out):
    out[...] = base[...]
    for s in range(ROUNDS * BT):
        out[:, lanes(send[s])] += (c0, c1, c2)[s // BT][:, tile_of(s % BT)].astype(f32)


def weights_kernel(slots, gws, gwn):
    for j in range(NZC):
        out, row = (gwn, j // 2 * 8) if j < 8 else (gws, j // 2 * 8 - FR)
        out[row : row + 8, tile_of(j % 2)] = slots[j].astype(f32)


def call(kernel, ins, outs, scratch=(), flops=0, nbytes=1 << 20, aliases=()):
    many = isinstance(outs, tuple)
    kinds = (VMEM, SMEM, pl.BlockSpec(memory_space=pl.ANY), VMEM)
    run = pl.pallas_call(
        kernel,
        out_shape=outs,
        in_specs=[kinds[i] for i in ins],
        out_specs=tuple(VMEM for _ in outs) if many else VMEM,
        scratch_shapes=list(scratch),
        input_output_aliases=dict(aliases),
        cost_estimate=pl.CostEstimate(flops=flops, bytes_accessed=nbytes, transcendentals=0),
    )

    def apply(*args):
        near = [
            a if i else pltpu.with_memory_space_constraint(a, pltpu.VMEM)
            for i, a in zip(ins, args, strict=True)
        ]
        return run(*near)

    return apply


def swap(x, axis):
    return lax.ppermute(x, axis, [(0, 1), (1, 0)])


def shards(x, ws, wn, in_adj, in_rows, in_cols, bnd_adj, bnd_send, bnd_rows, g):
    S, V = jax.ShapeDtypeStruct, pltpu.VMEM
    part = V((FR, LOCAL), bf16)
    sems = pltpu.SemaphoreType.DMA
    here, p2, p1, p0 = call(pick_kernel, (1, 3), (part,) * 4)(bnd_send, x)
    got = [swap(p, axis) for p, axis in zip((p2, p1, p0), PAIRS[::-1])]
    far = (in_adj, bnd_adj, ws, wn)
    in_adj, bnd_adj, ws, wn, give, acc = call(
        inner_kernel,
        (1, 1, 0) + (2,) * 5,
        tuple(V(a.shape, a.dtype) for a in far)
        + (V((NF, ROWS, LOCAL), bf16), V((TILES, FR, TILE), f32)),
        (V((HR, LOCAL), bf16), sems((5,))),
    )(in_rows, in_cols, here, *far, g)
    give = call(
        outer_kernel,
        (1,) + (0,) * 6,
        V((NF, ROWS, LOCAL), bf16),
        (V((TILES, FR, TILE), f32),),
        aliases=((6, 0),),
    )(bnd_rows, *got, bnd_adj, acc, give)
    block = lax.all_to_all(give, "f", 0, 0, tiled=True)
    y, own, ga, b0, b1, b2, slots = call(
        node_kernel,
        (1,) + (0,) * 4,
        (
            V((HR, LOCAL), bf16),
            V((TILES, FR, TILE), f32),
            V((TILES, FR, TILE), bf16),
            part,
            *(V((FR, LOCAL), f32),) * 2,
            S((NZC, 8, TILE), f32),
        ),
        (V((2 * F_IN, F_HID), bf16), V((2 * F_IN, LOCAL), bf16), V((F_HID, LOCAL), f32)),
    )(bnd_rows, block, ws, wn, bnd_adj)
    slots = lax.all_to_all(slots, ZC, 0, 0, tiled=True)
    c2 = swap(b2, PAIRS[2])
    base, y = call(
        back_kernel,
        (1, 1) + (0,) * 4,
        (V((FR, LOCAL), f32), S((HR, LOCAL), bf16)),
        (V((TILES, FR, TILE), f32),),
    )(in_rows, in_cols, own, ga, in_adj, y)
    slots, base, b1 = lax.optimization_barrier((slots, base, b1))
    c1 = swap(b1, PAIRS[1])
    terms = call(sum_kernel, (0,), S((NY, 8, TILE), f32))(slots)
    terms = lax.all_to_all(terms, Y, 0, 0, tiled=True)
    terms, c2, b0 = lax.optimization_barrier((terms, c2, b0))
    c0 = swap(b0, PAIRS[0])
    slots = call(sum_kernel, (0,), S((NZC, 8, TILE), bf16))(terms)
    slots = lax.all_to_all(slots, ZC, 0, 0, tiled=True)
    gx = call(grad_x_kernel, (1, 0, 0, 0, 0), S((FR, LOCAL), f32))(bnd_send, base, c0, c1, c2)
    half = S((FR, F_HID), f32)
    gws, gwn = call(weights_kernel, (0,), (half, half))(slots)
    return y, gx, gws, gwn


def solution(mesh):
    fine = Mesh(mesh.devices.reshape(SIZES), AXES)
    in_specs = (
        P("f", DOM),
        P("f", None),
        P("f", None),
        P(DOM, None, None),
        P(DOM),
        P(DOM),
        P(DOM, None, None),
        P(DOM),
        P(DOM),
        P("f", DOM),
    )
    out_specs = (P("f", DOM), P("f", DOM), P("f", None), P("f", None))
    return jax.shard_map(shards, mesh=fine, in_specs=in_specs, out_specs=out_specs, check_vma=False)
```

```python
import math

import jax
import jax.numpy as jnp
from jax import lax
from jax.experimental import pallas as pl
from jax.experimental.pallas import tpu as pltpu
from jax.sharding import Mesh
from jax.sharding import PartitionSpec as P

F_IN = 128
F_HID = 256
TILE = 128
TILES = 4
ROUNDS = 3
BT = 4
KIN = 12
NODES = 65536
NF = 4
FR = F_IN // NF
HR = F_HID // NF
LOCAL = TILES * TILE
EPS = 1e-05

AXES = ("y2", "yl", "z2", "z1", "z0", "c", "f")
SIZES = (2, 4, 2, 2, 2, 2, 4)
DOM = AXES[:6]
Y = ("y2", "yl")
NY = 8
ZC = ("z2", "z1", "z0", "c")
NZC = 16
PAIRS = ("z0", "z2", "y2")

R_AGG, R_X, R_G, R_W = 0, FR, 2 * FR, 2 * FR + HR
ROWS = R_W + FR

SMEM = pl.BlockSpec(memory_space=pltpu.SMEM)
VMEM = pl.BlockSpec(memory_space=pltpu.VMEM)
f32, bf16 = jnp.float32, jnp.bfloat16


def lanes(tile):
    return pl.ds(pl.multiple_of(tile * TILE, TILE), TILE)


def tile_of(b):
    return slice(b * TILE, (b + 1) * TILE)


def pick_kernel(send, x, here, o2, o1, o0):
    here[...] = x[...]
    for r, out in enumerate((o0, o1, o2)):
        for b in range(BT):
            out[:, tile_of(b)] = x[:, lanes(send[r * BT + b])]


NT = (((1,), (1,)), ((), ()))


def inner_kernel(rows, cols, x, *refs):
    far, near, (give, acc, g, sem) = refs[:5], refs[5:9], refs[9:]
    adj, badj, ws, wn = near
    copies = [
        pltpu.make_async_copy(a, b, sem.at[i])
        for i, (a, b) in enumerate(zip(far, (*near, g), strict=True))
    ]
    for copy in copies:
        copy.start()
    acc[...] = jnp.zeros_like(acc)
    for i in range(NF):
        give[i, R_X : R_X + FR, :] = x[...]
    copies[0].wait()
    for k in range(KIN):
        acc[rows[k]] += lax.dot_general(
            x[:, lanes(cols[k])], adj[k], NT, preferred_element_type=f32
        )
    for copy in copies[1:]:
        copy.wait()
    for i in range(NF):
        give[i, R_G : R_G + HR, :] = g[...]
        give[i, R_W : R_W + FR, :F_HID] = ws[...]
        give[i, R_W : R_W + FR, F_HID:] = wn[...]


def outer_kernel(brows, r2, r1, r0, badj, inner, half, give, acc):
    del half
    acc[...] = inner[...]
    got = (r0, r1, r2)
    for s in range(ROUNDS * BT):
        acc[brows[s]] += lax.dot_general(
            got[s // BT][:, tile_of(s % BT)], badj[s], NT, preferred_element_type=f32
        )
    for t in range(TILES):
        part = acc[t].astype(bf16)
        for i in range(NF):
            give[i, R_AGG : R_AGG + FR, tile_of(t)] = part


def node_kernel(brows, got, ws, wn, badj, y, acc, ga, b0, b1, b2, slots, lhs, rhs, act_all):
    for i in range(NF):
        lhs[i * FR : (i + 1) * FR, :] = got[i, R_W : R_W + FR, :F_HID]
        lhs[F_IN + i * FR : F_IN + (i + 1) * FR, :] = got[i, R_W : R_W + FR, F_HID:]
        rhs[i * FR : (i + 1) * FR, :] = got[i, R_X : R_X + FR, :]
        rhs[F_IN + i * FR : F_IN + (i + 1) * FR, :] = got[i, R_AGG : R_AGG + FR, :]
    tn = (((0,), (0,)), ((), ()))
    pre = lax.dot_general(lhs[...], rhs[...], tn, preferred_element_type=f32)
    gate = 1.0 / (1.0 + jnp.exp(-pre))
    act = pre * gate
    act_all[...] = act
    g = jnp.concatenate([got[i, R_G : R_G + HR, :] for i in range(NF)], axis=0).astype(f32)
    sq = jnp.sum(act * act, axis=0, keepdims=True)
    al = jnp.sum(g * act, axis=0, keepdims=True)
    rs = lax.rsqrt(sq / F_HID + EPS)
    coef = rs * rs * rs * (al / F_HID)
    grad_act = rs * g - act * coef
    grad = (grad_act * gate * (1.0 + pre * (1.0 - gate))).astype(bf16)
    f = lax.axis_index("f")
    y[...] = (act_all[pl.ds(pl.multiple_of(f * HR, HR), HR), :] * rs).astype(bf16)
    w = lax.dot_general(
        got[f, R_AGG : R_AGG + 2 * FR, :], grad, (((1,), (1,)), ((), ())), preferred_element_type=f32
    ) * (1.0 / math.sqrt(NODES))
    for j in range(NZC):
        slots[j] = w[j // 2 * 8 : j // 2 * 8 + 8, tile_of(j % 2)]
    both = jnp.dot(
        jnp.concatenate([ws[...], wn[...]], axis=0), grad, preferred_element_type=f32
    )
    for t in range(TILES):
        acc[t] = both[:FR, tile_of(t)]
        ga[t] = both[FR:, tile_of(t)].astype(bf16)
    outs = (b0, b1, b2)
    for s in range(ROUNDS * BT):
        r, b = divmod(s, BT)
        outs[r][:, tile_of(b)] = jnp.dot(ga[brows[s]], badj[s], preferred_element_type=f32)


def sum_kernel(terms, out):
    total = terms[0]
    for j in range(1, terms.shape[0]):
        total += terms[j]
    for j in range(out.shape[0]):
        out[j] = total.astype(out.dtype)


def grad_x_kernel(rows, cols, send, own, ga, adj, c0, c1, c2, y, out, y_out, acc):
    y_out[...] = y[...]
    acc[...] = own[...]
    for k in range(KIN):
        acc[cols[k]] += jnp.dot(ga[rows[k]], adj[k], preferred_element_type=f32)
    for s in range(ROUNDS * BT):
        acc[send[s]] += (c0, c1, c2)[s // BT][:, tile_of(s % BT)]
    for t in range(TILES):
        out[:, tile_of(t)] = acc[t]


def weights_kernel(slots, gws, gwn):
    for j in range(NZC):
        out, row = (gwn, j // 2 * 8) if j < 8 else (gws, j // 2 * 8 - FR)
        out[row : row + 8, tile_of(j % 2)] = slots[j].astype(f32)


def call(kernel, ins, outs, scratch=(), flops=0, nbytes=1 << 20, aliases=()):
    many = isinstance(outs, tuple)
    kinds = (VMEM, SMEM, pl.BlockSpec(memory_space=pl.ANY), VMEM)
    run = pl.pallas_call(
        kernel,
        out_shape=outs,
        in_specs=[kinds[i] for i in ins],
        out_specs=tuple(VMEM for _ in outs) if many else VMEM,
        scratch_shapes=list(scratch),
        input_output_aliases=dict(aliases),
        cost_estimate=pl.CostEstimate(flops=flops, bytes_accessed=nbytes, transcendentals=0),
    )

    def apply(*args):
        near = [
            a if i else pltpu.with_memory_space_constraint(a, pltpu.VMEM)
            for i, a in zip(ins, args, strict=True)
        ]
        return run(*near)

    return apply


def swap(x, axis):
    return lax.ppermute(x, axis, [(0, 1), (1, 0)])


def shards(x, ws, wn, in_adj, in_rows, in_cols, bnd_adj, bnd_send, bnd_rows, g):
    S, V = jax.ShapeDtypeStruct, pltpu.VMEM
    part = V((FR, LOCAL), bf16)
    sems = pltpu.SemaphoreType.DMA
    here, p2, p1, p0 = call(pick_kernel, (1, 3), (part,) * 4)(bnd_send, x)
    got = [swap(p, axis) for p, axis in zip((p2, p1, p0), PAIRS[::-1])]
    far = (in_adj, bnd_adj, ws, wn)
    in_adj, bnd_adj, ws, wn, give, acc = call(
        inner_kernel,
        (1, 1, 0) + (2,) * 5,
        tuple(V(a.shape, a.dtype) for a in far)
        + (V((NF, ROWS, LOCAL), bf16), V((TILES, FR, TILE), f32)),
        (V((HR, LOCAL), bf16), sems((5,))),
    )(in_rows, in_cols, here, *far, g)
    give = call(
        outer_kernel,
        (1,) + (0,) * 6,
        V((NF, ROWS, LOCAL), bf16),
        (V((TILES, FR, TILE), f32),),
        aliases=((6, 0),),
    )(bnd_rows, *got, bnd_adj, acc, give)
    block = lax.all_to_all(give, "f", 0, 0, tiled=True)
    y, own, ga, b0, b1, b2, slots = call(
        node_kernel,
        (1,) + (0,) * 4,
        (
            V((HR, LOCAL), bf16),
            V((TILES, FR, TILE), f32),
            V((TILES, FR, TILE), bf16),
            *(V((FR, LOCAL), f32),) * 3,
            S((NZC, 8, TILE), f32),
        ),
        (V((2 * F_IN, F_HID), bf16), V((2 * F_IN, LOCAL), bf16), V((F_HID, LOCAL), f32)),
    )(bnd_rows, block, ws, wn, bnd_adj)
    slots = lax.all_to_all(slots, ZC, 0, 0, tiled=True)
    c2 = swap(b2, PAIRS[2])
    c0 = swap(b0, PAIRS[0])
    slots, b1 = lax.optimization_barrier((slots, b1))
    c1 = swap(b1, PAIRS[1])
    terms = call(sum_kernel, (0,), S((NY, 8, TILE), f32))(slots)
    terms = lax.all_to_all(terms, Y, 0, 0, tiled=True)
    terms, c2, c0, own = lax.optimization_barrier((terms, c2, c0, own))
    slots = call(sum_kernel, (0,), S((NZC, 8, TILE), bf16))(terms)
    slots = lax.all_to_all(slots, ZC, 0, 0, tiled=True)
    gx, y = call(
        grad_x_kernel,
        (1, 1, 1) + (0,) * 7,
        (S((FR, LOCAL), f32), S((HR, LOCAL), bf16)),
        (V((TILES, FR, TILE), f32),),
    )(in_rows, in_cols, bnd_send, own, ga, in_adj, c0, c1, c2, y)
    half = S((FR, F_HID), f32)
    gws, gwn = call(weights_kernel, (0,), (half, half))(slots)
    return y, gx, gws, gwn


def solution(mesh):
    fine = Mesh(mesh.devices.reshape(SIZES), AXES)
    in_specs = (
        P("f", DOM),
        P("f", None),
        P("f", None),
        P(DOM, None, None),
        P(DOM),
        P(DOM),
        P(DOM, None, None),
        P(DOM),
        P(DOM),
        P("f", DOM),
    )
    out_specs = (P("f", DOM), P("f", DOM), P("f", None), P("f", None))
    return jax.shard_map(shards, mesh=fine, in_specs=in_specs, out_specs=out_specs, check_vma=False)
```

```python
import math

import jax
import jax.numpy as jnp
from jax import lax
from jax.experimental import pallas as pl
from jax.experimental.pallas import tpu as pltpu
from jax.sharding import Mesh
from jax.sharding import PartitionSpec as P

F_IN = 128
F_HID = 256
TILE = 128
TILES = 4
ROUNDS = 3
BT = 4
KIN = 12
NODES = 65536
NF = 4
FR = F_IN // NF
HR = F_HID // NF
LOCAL = TILES * TILE
EPS = 1e-05

AXES = ("y2", "yl", "z2", "z1", "z0", "c", "f")
SIZES = (2, 4, 2, 2, 2, 2, 4)
DOM = AXES[:6]
Y = ("y2", "yl")
NY = 8
ZC = ("z2", "z1", "z0", "c")
NZC = 16
PAIRS = ("z0", "z2", "y2")

R_AGG, R_X, R_G, R_W = 0, FR, 2 * FR, 2 * FR + HR
ROWS = R_W + FR

SMEM = pl.BlockSpec(memory_space=pltpu.SMEM)
VMEM = pl.BlockSpec(memory_space=pltpu.VMEM)
f32, bf16 = jnp.float32, jnp.bfloat16


def lanes(tile):
    return pl.ds(pl.multiple_of(tile * TILE, TILE), TILE)


def tile_of(b):
    return slice(b * TILE, (b + 1) * TILE)


def pick_kernel(send, x, here, o2, o1, o0):
    here[...] = x[...]
    for r, out in enumerate((o0, o1, o2)):
        for b in range(BT):
            out[:, tile_of(b)] = x[:, lanes(send[r * BT + b])]


NT = (((1,), (1,)), ((), ()))


def inner_kernel(rows, cols, x, *refs):
    far, near, (give, acc, g, sem) = refs[:5], refs[5:9], refs[9:]
    adj, badj, ws, wn = near
    copies = [
        pltpu.make_async_copy(a, b, sem.at[i])
        for i, (a, b) in enumerate(zip(far, (*near, g), strict=True))
    ]
    for copy in copies:
        copy.start()
    acc[...] = jnp.zeros_like(acc)
    for i in range(NF):
        give[i, R_X : R_X + FR, :] = x[...]
    copies[0].wait()
    for k in range(KIN):
        acc[rows[k]] += lax.dot_general(
            x[:, lanes(cols[k])], adj[k], NT, preferred_element_type=f32
        )
    for copy in copies[1:]:
        copy.wait()
    for i in range(NF):
        give[i, R_G : R_G + HR, :] = g[...]
        give[i, R_W : R_W + FR, :F_HID] = ws[...]
        give[i, R_W : R_W + FR, F_HID:] = wn[...]


def outer_kernel(brows, r2, r1, r0, badj, inner, half, give, acc):
    del half
    acc[...] = inner[...]
    got = (r0, r1, r2)
    for s in range(ROUNDS * BT):
        acc[brows[s]] += lax.dot_general(
            got[s // BT][:, tile_of(s % BT)], badj[s], NT, preferred_element_type=f32
        )
    for t in range(TILES):
        part = acc[t].astype(bf16)
        for i in range(NF):
            give[i, R_AGG : R_AGG + FR, tile_of(t)] = part


def node_kernel(brows, got, ws, wn, badj, y, acc, ga, b0, b1, b2, slots, lhs, rhs, act_all):
    for i in range(NF):
        lhs[i * FR : (i + 1) * FR, :] = got[i, R_W : R_W + FR, :F_HID]
        lhs[F_IN + i * FR : F_IN + (i + 1) * FR, :] = got[i, R_W : R_W + FR, F_HID:]
        rhs[i * FR : (i + 1) * FR, :] = got[i, R_X : R_X + FR, :]
        rhs[F_IN + i * FR : F_IN + (i + 1) * FR, :] = got[i, R_AGG : R_AGG + FR, :]
    tn = (((0,), (0,)), ((), ()))
    pre = lax.dot_general(lhs[...], rhs[...], tn, preferred_element_type=f32)
    gate = 1.0 / (1.0 + jnp.exp(-pre))
    act = pre * gate
    act_all[...] = act
    g = jnp.concatenate([got[i, R_G : R_G + HR, :] for i in range(NF)], axis=0).astype(f32)
    sq = jnp.sum(act * act, axis=0, keepdims=True)
    al = jnp.sum(g * act, axis=0, keepdims=True)
    rs = lax.rsqrt(sq / F_HID + EPS)
    coef = rs * rs * rs * (al / F_HID)
    grad_act = rs * g - act * coef
    grad = (grad_act * gate * (1.0 + pre * (1.0 - gate))).astype(bf16)
    f = lax.axis_index("f")
    y[...] = (act_all[pl.ds(pl.multiple_of(f * HR, HR), HR), :] * rs).astype(bf16)
    w = lax.dot_general(
        got[f, R_AGG : R_AGG + 2 * FR, :], grad, (((1,), (1,)), ((), ())), preferred_element_type=f32
    ) * (1.0 / math.sqrt(NODES))
    for j in range(NZC):
        slots[j] = w[j // 2 * 8 : j // 2 * 8 + 8, tile_of(j % 2)]
    both = jnp.dot(
        jnp.concatenate([ws[...], wn[...]], axis=0), grad, preferred_element_type=f32
    )
    for t in range(TILES):
        acc[t] = both[:FR, tile_of(t)]
        ga[t] = both[FR:, tile_of(t)].astype(bf16)
    outs = (b0, b1, b2)
    for s in range(ROUNDS * BT):
        r, b = divmod(s, BT)
        outs[r][:, tile_of(b)] = jnp.dot(
            ga[brows[s]], badj[s], preferred_element_type=f32
        ).astype(outs[r].dtype)


def back_kernel(rows, cols, own, ga, adj, y, base, out, acc):
    out[...] = y[...]
    acc[...] = own[...]
    for k in range(KIN):
        acc[cols[k]] += jnp.dot(ga[rows[k]], adj[k], preferred_element_type=f32)
    base[...] = acc[...]


def sum_kernel(terms, out):
    total = terms[0]
    for j in range(1, terms.shape[0]):
        total += terms[j]
    for j in range(out.shape[0]):
        out[j] = total.astype(out.dtype)


def far_kernel(send, base, c1, c2, out):
    out[...] = base[...]
    for s in range(BT, ROUNDS * BT):
        out[send[s]] += (c1, c2)[s // BT - 1][:, tile_of(s % BT)].astype(f32)


def last_kernel(send, base, c0, slots, gx, gws, gwn, acc):
    for j in range(NZC):
        out, row = (gwn, j // 2 * 8) if j < 8 else (gws, j // 2 * 8 - FR)
        out[row : row + 8, tile_of(j % 2)] = slots[j].astype(f32)
    acc[...] = base[...]
    for s in range(BT):
        acc[send[s]] += c0[:, tile_of(s)].astype(f32)
    for t in range(TILES):
        gx[:, tile_of(t)] = acc[t]


def call(kernel, ins, outs, scratch=(), flops=0, nbytes=1 << 20, aliases=()):
    many = isinstance(outs, tuple)
    kinds = (VMEM, SMEM, pl.BlockSpec(memory_space=pl.ANY), VMEM)
    run = pl.pallas_call(
        kernel,
        out_shape=outs,
        in_specs=[kinds[i] for i in ins],
        out_specs=tuple(VMEM for _ in outs) if many else VMEM,
        scratch_shapes=list(scratch),
        input_output_aliases=dict(aliases),
        cost_estimate=pl.CostEstimate(flops=flops, bytes_accessed=nbytes, transcendentals=0),
    )

    def apply(*args):
        near = [
            a if i else pltpu.with_memory_space_constraint(a, pltpu.VMEM)
            for i, a in zip(ins, args, strict=True)
        ]
        return run(*near)

    return apply


def swap(x, axis):
    return lax.ppermute(x, axis, [(0, 1), (1, 0)])


def shards(x, ws, wn, in_adj, in_rows, in_cols, bnd_adj, bnd_send, bnd_rows, g):
    S, V = jax.ShapeDtypeStruct, pltpu.VMEM
    part = V((FR, LOCAL), bf16)
    sems = pltpu.SemaphoreType.DMA
    here, p2, p1, p0 = call(pick_kernel, (1, 3), (part,) * 4)(bnd_send, x)
    got = [swap(p, axis) for p, axis in zip((p2, p1, p0), PAIRS[::-1])]
    far = (in_adj, bnd_adj, ws, wn)
    in_adj, bnd_adj, ws, wn, give, acc = call(
        inner_kernel,
        (1, 1, 0) + (2,) * 5,
        tuple(V(a.shape, a.dtype) for a in far)
        + (V((NF, ROWS, LOCAL), bf16), V((TILES, FR, TILE), f32)),
        (V((HR, LOCAL), bf16), sems((5,))),
    )(in_rows, in_cols, here, *far, g)
    give = call(
        outer_kernel,
        (1,) + (0,) * 6,
        V((NF, ROWS, LOCAL), bf16),
        (V((TILES, FR, TILE), f32),),
        aliases=((6, 0),),
    )(bnd_rows, *got, bnd_adj, acc, give)
    block = lax.all_to_all(give, "f", 0, 0, tiled=True)
    y, own, ga, b0, b1, b2, slots = call(
        node_kernel,
        (1,) + (0,) * 4,
        (
            V((HR, LOCAL), bf16),
            V((TILES, FR, TILE), f32),
            V((TILES, FR, TILE), bf16),
            part,
            *(V((FR, LOCAL), f32),) * 2,
            S((NZC, 8, TILE), f32),
        ),
        (V((2 * F_IN, F_HID), bf16), V((2 * F_IN, LOCAL), bf16), V((F_HID, LOCAL), f32)),
    )(bnd_rows, block, ws, wn, bnd_adj)
    slots = lax.all_to_all(slots, ZC, 0, 0, tiled=True)
    c2 = swap(b2, PAIRS[2])
    base, y = call(
        back_kernel,
        (1, 1) + (0,) * 4,
        (V((TILES, FR, TILE), f32), S((HR, LOCAL), bf16)),
        (V((TILES, FR, TILE), f32),),
    )(in_rows, in_cols, own, ga, in_adj, y)
    slots, base, b1 = lax.optimization_barrier((slots, base, b1))
    c1 = swap(b1, PAIRS[1])
    terms = call(sum_kernel, (0,), S((NY, 8, TILE), f32))(slots)
    terms = lax.all_to_all(terms, Y, 0, 0, tiled=True)
    terms, c2, b0 = lax.optimization_barrier((terms, c2, b0))
    c0 = swap(b0, PAIRS[0])
    slots = call(sum_kernel, (0,), S((NZC, 8, TILE), bf16))(terms)
    slots = lax.all_to_all(slots, ZC, 0, 0, tiled=True)
    base = call(far_kernel, (1, 0, 0, 0), V((TILES, FR, TILE), f32))(bnd_send, base, c1, c2)
    half = S((FR, F_HID), f32)
    gx, gws, gwn = call(
        last_kernel,
        (1, 0, 0, 0),
        (S((FR, LOCAL), f32), half, half),
        (V((TILES, FR, TILE), f32),),
    )(bnd_send, base, c0, slots)
    return y, gx, gws, gwn


def solution(mesh):
    fine = Mesh(mesh.devices.reshape(SIZES), AXES)
    in_specs = (
        P("f", DOM),
        P("f", None),
        P("f", None),
        P(DOM, None, None),
        P(DOM),
        P(DOM),
        P(DOM, None, None),
        P(DOM),
        P(DOM),
        P("f", DOM),
    )
    out_specs = (P("f", DOM), P("f", DOM), P("f", None), P("f", None))
    return jax.shard_map(shards, mesh=fine, in_specs=in_specs, out_specs=out_specs, check_vma=False)
```

```python
import math

import jax
import jax.numpy as jnp
from jax import lax
from jax.experimental import pallas as pl
from jax.experimental.pallas import tpu as pltpu
from jax.sharding import Mesh
from jax.sharding import PartitionSpec as P

F_IN = 128
F_HID = 256
TILE = 128
TILES = 4
ROUNDS = 3
BT = 4
KIN = 12
NODES = 65536
NF = 4
FR = F_IN // NF
HR = F_HID // NF
LOCAL = TILES * TILE
EPS = 1e-05

AXES = ("y2", "yl", "z2", "z1", "z0", "c", "f")
SIZES = (2, 4, 2, 2, 2, 2, 4)
DOM = AXES[:6]
Y = ("yl", "y2")
NY = 8
ZC = ("c", "z2", "z1", "z0")
NZC = 16
PAIRS = ("z0", "z2", "y2")

R_AGG, R_X, R_G, R_W = 0, FR, 2 * FR, 2 * FR + HR
ROWS = R_W + FR

SMEM = pl.BlockSpec(memory_space=pltpu.SMEM)
VMEM = pl.BlockSpec(memory_space=pltpu.VMEM)
f32, bf16 = jnp.float32, jnp.bfloat16


def lanes(tile):
    return pl.ds(pl.multiple_of(tile * TILE, TILE), TILE)


def tile_of(b):
    return slice(b * TILE, (b + 1) * TILE)


def pick_kernel(send, x, here, o2, o1, o0):
    here[...] = x[...]
    for r, out in enumerate((o0, o1, o2)):
        for b in range(BT):
            out[:, tile_of(b)] = x[:, lanes(send[r * BT + b])]


NT = (((1,), (1,)), ((), ()))


def inner_kernel(rows, cols, x, *refs):
    far, near, (give, acc, g, sem) = refs[:5], refs[5:9], refs[9:]
    adj, badj, ws, wn = near
    copies = [
        pltpu.make_async_copy(a, b, sem.at[i])
        for i, (a, b) in enumerate(zip(far, (*near, g), strict=True))
    ]
    for copy in copies:
        copy.start()
    acc[...] = jnp.zeros_like(acc)
    for i in range(NF):
        give[i, R_X : R_X + FR, :] = x[...]
    copies[0].wait()
    for k in range(KIN):
        acc[rows[k]] += lax.dot_general(
            x[:, lanes(cols[k])], adj[k], NT, preferred_element_type=f32
        )
    for copy in copies[1:]:
        copy.wait()
    for i in range(NF):
        give[i, R_G : R_G + HR, :] = g[...]
        give[i, R_W : R_W + FR, :F_HID] = ws[...]
        give[i, R_W : R_W + FR, F_HID:] = wn[...]


def outer_kernel(brows, r2, r1, r0, badj, inner, half, give, acc):
    del half
    acc[...] = inner[...]
    got = (r0, r1, r2)
    for s in range(ROUNDS * BT):
        acc[brows[s]] += lax.dot_general(
            got[s // BT][:, tile_of(s % BT)], badj[s], NT, preferred_element_type=f32
        )
    for t in range(TILES):
        part = acc[t].astype(bf16)
        for i in range(NF):
            give[i, R_AGG : R_AGG + FR, tile_of(t)] = part


def node_kernel(brows, got, ws, wn, badj, y, acc, ga, b0, b1, b2, slots, lhs, rhs, act_all):
    for i in range(NF):
        lhs[i * FR : (i + 1) * FR, :] = got[i, R_W : R_W + FR, :F_HID]
        lhs[F_IN + i * FR : F_IN + (i + 1) * FR, :] = got[i, R_W : R_W + FR, F_HID:]
        rhs[i * FR : (i + 1) * FR, :] = got[i, R_X : R_X + FR, :]
        rhs[F_IN + i * FR : F_IN + (i + 1) * FR, :] = got[i, R_AGG : R_AGG + FR, :]
    tn = (((0,), (0,)), ((), ()))
    pre = lax.dot_general(lhs[...], rhs[...], tn, preferred_element_type=f32)
    gate = 1.0 / (1.0 + jnp.exp(-pre))
    act = pre * gate
    act_all[...] = act
    g = jnp.concatenate([got[i, R_G : R_G + HR, :] for i in range(NF)], axis=0).astype(f32)
    sq = jnp.sum(act * act, axis=0, keepdims=True)
    al = jnp.sum(g * act, axis=0, keepdims=True)
    rs = lax.rsqrt(sq / F_HID + EPS)
    coef = rs * rs * rs * (al / F_HID)
    grad_act = rs * g - act * coef
    grad = (grad_act * gate * (1.0 + pre * (1.0 - gate))).astype(bf16)
    f = lax.axis_index("f")
    y[...] = (act_all[pl.ds(pl.multiple_of(f * HR, HR), HR), :] * rs).astype(bf16)
    w = lax.dot_general(
        got[f, R_AGG : R_AGG + 2 * FR, :], grad, (((1,), (1,)), ((), ())), preferred_element_type=f32
    ) * (1.0 / math.sqrt(NODES))
    for j in range(NZC):
        slots[j] = w[j // 2 * 8 : j // 2 * 8 + 8, tile_of(j % 2)]
    both = jnp.dot(
        jnp.concatenate([ws[...], wn[...]], axis=0), grad, preferred_element_type=f32
    )
    for t in range(TILES):
        acc[t] = both[:FR, tile_of(t)]
        ga[t] = both[FR:, tile_of(t)].astype(bf16)
    outs = (b0, b1, b2)
    for s in range(ROUNDS * BT):
        r, b = divmod(s, BT)
        outs[r][:, tile_of(b)] = jnp.dot(
            ga[brows[s]], badj[s], preferred_element_type=f32
        ).astype(outs[r].dtype)


def back_kernel(rows, cols, own, ga, adj, y, base, out, acc):
    out[...] = y[...]
    acc[...] = own[...]
    for k in range(KIN):
        acc[cols[k]] += jnp.dot(ga[rows[k]], adj[k], preferred_element_type=f32)
    for t in range(TILES):
        base[:, tile_of(t)] = acc[t]


def sum_kernel(terms, out):
    total = terms[0]
    for j in range(1, terms.shape[0]):
        total += terms[j]
    for j in range(out.shape[0]):
        out[j] = total.astype(out.dtype)


def grad_x_kernel(send, base, c0, c1, c2, out):
    out[...] = base[...]
    for s in range(ROUNDS * BT):
        out[:, lanes(send[s])] += (c0, c1, c2)[s // BT][:, tile_of(s % BT)].astype(f32)


def weights_kernel(slots, gws, gwn):
    for j in range(NZC):
        out, row = (gwn, j // 2 * 8) if j < 8 else (gws, j // 2 * 8 - FR)
        out[row : row + 8, tile_of(j % 2)] = slots[j].astype(f32)


def call(kernel, ins, outs, scratch=(), flops=0, nbytes=1 << 20, aliases=()):
    many = isinstance(outs, tuple)
    kinds = (VMEM, SMEM, pl.BlockSpec(memory_space=pl.ANY), VMEM)
    run = pl.pallas_call(
        kernel,
        out_shape=outs,
        in_specs=[kinds[i] for i in ins],
        out_specs=tuple(VMEM for _ in outs) if many else VMEM,
        scratch_shapes=list(scratch),
        input_output_aliases=dict(aliases),
        cost_estimate=pl.CostEstimate(flops=flops, bytes_accessed=nbytes, transcendentals=0),
    )

    def apply(*args):
        near = [
            a if i else pltpu.with_memory_space_constraint(a, pltpu.VMEM)
            for i, a in zip(ins, args, strict=True)
        ]
        return run(*near)

    return apply


def swap(x, axis):
    return lax.ppermute(x, axis, [(0, 1), (1, 0)])


def shards(x, ws, wn, in_adj, in_rows, in_cols, bnd_adj, bnd_send, bnd_rows, g):
    S, V = jax.ShapeDtypeStruct, pltpu.VMEM
    part = V((FR, LOCAL), bf16)
    sems = pltpu.SemaphoreType.DMA
    here, p2, p1, p0 = call(pick_kernel, (1, 3), (part,) * 4)(bnd_send, x)
    got = [swap(p, axis) for p, axis in zip((p2, p1, p0), PAIRS[::-1])]
    far = (in_adj, bnd_adj, ws, wn)
    in_adj, bnd_adj, ws, wn, give, acc = call(
        inner_kernel,
        (1, 1, 0) + (2,) * 5,
        tuple(V(a.shape, a.dtype) for a in far)
        + (V((NF, ROWS, LOCAL), bf16), V((TILES, FR, TILE), f32)),
        (V((HR, LOCAL), bf16), sems((5,))),
    )(in_rows, in_cols, here, *far, g)
    give = call(
        outer_kernel,
        (1,) + (0,) * 6,
        V((NF, ROWS, LOCAL), bf16),
        (V((TILES, FR, TILE), f32),),
        aliases=((6, 0),),
    )(bnd_rows, *got, bnd_adj, acc, give)
    block = lax.all_to_all(give, "f", 0, 0, tiled=True)
    y, own, ga, b0, b1, b2, slots = call(
        node_kernel,
        (1,) + (0,) * 4,
        (
            V((HR, LOCAL), bf16),
            V((TILES, FR, TILE), f32),
            V((TILES, FR, TILE), bf16),
            part,
            *(V((FR, LOCAL), f32),) * 2,
            S((NZC, 8, TILE), f32),
        ),
        (V((2 * F_IN, F_HID), bf16), V((2 * F_IN, LOCAL), bf16), V((F_HID, LOCAL), f32)),
    )(bnd_rows, block, ws, wn, bnd_adj)
    slots = lax.all_to_all(slots, ZC, 0, 0, tiled=True)
    c2 = swap(b2, PAIRS[2])
    base, y = call(
        back_kernel,
        (1, 1) + (0,) * 4,
        (V((FR, LOCAL), f32), S((HR, LOCAL), bf16)),
        (V((TILES, FR, TILE), f32),),
    )(in_rows, in_cols, own, ga, in_adj, y)
    slots, base, b1 = lax.optimization_barrier((slots, base, b1))
    c1 = swap(b1, PAIRS[1])
    terms = call(sum_kernel, (0,), S((NY, 8, TILE), f32))(slots)
    terms = lax.all_to_all(terms, Y, 0, 0, tiled=True)
    terms, c2, b0 = lax.optimization_barrier((terms, c2, b0))
    c0 = swap(b0, PAIRS[0])
    slots = call(sum_kernel, (0,), S((NZC, 8, TILE), bf16))(terms)
    slots = lax.all_to_all(slots, ZC, 0, 0, tiled=True)
    gx = call(grad_x_kernel, (1, 0, 0, 0, 0), S((FR, LOCAL), f32))(bnd_send, base, c0, c1, c2)
    half = S((FR, F_HID), f32)
    gws, gwn = call(weights_kernel, (0,), (half, half))(slots)
    return y, gx, gws, gwn


def solution(mesh):
    fine = Mesh(mesh.devices.reshape(SIZES), AXES)
    in_specs = (
        P("f", DOM),
        P("f", None),
        P("f", None),
        P(DOM, None, None),
        P(DOM),
        P(DOM),
        P(DOM, None, None),
        P(DOM),
        P(DOM),
        P("f", DOM),
    )
    out_specs = (P("f", DOM), P("f", DOM), P("f", None), P("f", None))
    return jax.shard_map(shards, mesh=fine, in_specs=in_specs, out_specs=out_specs, check_vma=False)
```
